512 devices in a mesh: dp: 16 (over z), head: 8 (over x, core), srv: 4 (over y).
Axes of the slice: x: 4, y: 4, z: 16, core: 2. Of those that a mesh axis runs over, the one named last changes fastest.
Arguments:
- queries: bfloat16 [2048, 8, 1024], P('dp', 'srv', 'head'), may hold values from -5 to 5
- keys: bfloat16 [10240, 1024], P(('dp', 'head')), may hold values from -5 to 5
- values: bfloat16 [10240, 1024], P(('dp', 'head')), may hold values from -6 to 6
- output_gradient: bfloat16 [2048, 8, 1024], P('dp', 'srv', 'head'), may hold values from -6 to 6
- doc_ids: int32 [10240], P('dp'), may hold values from 0 to 7, never falling along the last dimension, each value on 1 to 5120 neighbouring positions
Outputs:
- attention: bfloat16 [2048, 8, 1024], P('dp', 'srv', 'head')
- q_grad: bfloat16 [2048, 8, 1024], P('dp', 'srv', 'head')
- k_grad: bfloat16 [10240, 1024], P(('dp', 'head', 'srv'))
- v_grad: bfloat16 [10240, 1024], P(('dp', 'head', 'srv'))
The draws below stay inside these ranges and needn't reach their ends.
Inputs may be any that keep to these rules, and one draw needn't show every extreme that they name: `doc_ids`: document numbers never fall along the keys; every document holds at most 5120 keys, and one holds exactly 5120.
All inputs are finite; a program needn't handle non-finite values.
Results may differ from the reference program's by a relative error of at most 0.039.
Values may be sent and summed in bfloat16 or wider, within the bound.
No kernel may reach another device: no remote copies, remote signals or barrier semaphores. Data moves between devices by JAX's collectives and lax.ppermute only.
A program may use at most 64 MiB of HBM per device.

```python
import math
import jax
import jax.numpy as jnp
import numpy as np
from jax import lax

HEAD_SIZE = 128
KEY_VALUE_HEADS = 8
QUERY_PER_KV = 8
DOCS = 8
QUERY_ROWS = 2048
CONTEXT_KEYS = 8192
KEYS_PER_SHARD = 640
KEY_TOTAL = 10240
DOC_MAX = 5120
N_DP = 16


def draw_queries(key, part):
    local_key_rows = jax.random.fold_in(key, 101)
    final_output = jnp.clip(jax.random.normal(local_key_rows, (QUERY_ROWS, QUERY_PER_KV, KEY_VALUE_HEADS * HEAD_SIZE), jnp.float32), -5.0, 5.0)
    return final_output.astype(jnp.bfloat16)


def draw_keys(key, part):
    local_key_rows = jax.random.fold_in(key, 202)
    final_output = jnp.clip(jax.random.normal(local_key_rows, (KEY_TOTAL, KEY_VALUE_HEADS * HEAD_SIZE), jnp.float32), -5.0, 5.0)
    return final_output.astype(jnp.bfloat16)


def shard_levels(stream_key, extent, pieces, least, high):
    gain = 1.0
    for dim, blocks in pieces:
        draws = jax.random.uniform(jax.random.fold_in(jax.random.fold_in(stream_key, 6), dim), (blocks,), jnp.float32, least / len(pieces), high / len(pieces))
        gain = gain * jnp.repeat(jnp.exp(draws), extent[dim] // blocks).reshape((-1,) + (1,) * (len(extent) - 1 - dim))
    return gain


def profile(amount, total, limit, slope):
    weights = [(1 << 20) // math.isqrt(standing ** slope) + 1 for standing in range(2, amount + 1)]
    surplus, holding = total - limit - (amount - 1), [1] * (amount - 1)
    while surplus > 0:
        free = [i for i in range(amount - 1) if holding[i] < limit]
        whole, budget = sum([weights[i] for i in free]), surplus
        for i in free:
            more = min(limit - holding[i], max(1, budget * weights[i] // whole), surplus)
            holding[i] = holding[i] + more
            surplus = surplus - more
    return np.array([limit] + holding)


def ragged_sizes(rng, amount, total, most, slope):
    if amount == 2:
        one = jax.random.randint(rng, (), max(1, total - most), min(most, total - 1) + 1)
        return jnp.stack([one, total - one])
    tallies = jnp.asarray(profile(amount, total, most, slope), jnp.int32)
    pairs = (amount - 1) // 2
    giver, sink = tallies[1:1 + 2 * pairs:2], tallies[2:2 + 2 * pairs:2]
    room = jnp.minimum(giver - 1, most - sink)
    shifted = jax.random.randint(jax.random.fold_in(rng, 1), (pairs,), 0, 1 << 20) % (room + 1)
    tallies = tallies.at[1:1 + 2 * pairs:2].set(giver - shifted).at[2:2 + 2 * pairs:2].set(sink + shifted)
    return tallies[jax.random.permutation(jax.random.fold_in(rng, 2), amount)]


def gaussian(rng, dims, scale, reach, shards=(), kind=jnp.bfloat16):
    loudness = shard_levels(rng, dims, shards, -0.22, 0.18) if shards else 1.0
    values = jax.random.normal(rng, dims, jnp.float32) * scale * loudness
    return jnp.minimum(jnp.maximum(values, -reach), reach).astype(kind)


def setup_inputs(seed: int = 0) -> dict:
    key_of = jax.random.split(jax.random.key(seed), 6)
    return {
        "queries": draw_queries(jax.random.fold_in(key_of[5], 71), 0),
        "keys": draw_keys(jax.random.fold_in(key_of[5], 71), 0),
        "values": gaussian(key_of[2], (KEY_TOTAL, KEY_VALUE_HEADS * HEAD_SIZE), 1.0, 6.0, ((0, 128),)),
        "output_gradient": gaussian(key_of[3], (QUERY_ROWS, QUERY_PER_KV, KEY_VALUE_HEADS * HEAD_SIZE), 1.0, 6.0, ((0, 16), (1, 4), (2, 8))),
        "doc_ids": jnp.searchsorted(jnp.cumsum(ragged_sizes(key_of[4], DOCS, KEY_TOTAL, DOC_MAX, 2)), jnp.arange(KEY_TOTAL), side="right").astype(jnp.int32),
    }


NEGATIVE = -1.0e30


def settle(array_f32):
    rounded = lax.optimization_barrier(array_f32.astype(jnp.bfloat16))
    return rounded.astype(jnp.float32)


def reference(queries, keys, values, output_gradient, doc_ids):
    scale_factor = HEAD_SIZE ** -0.5
    query_head_rows = queries.astype(jnp.float32).reshape(QUERY_ROWS, QUERY_PER_KV, KEY_VALUE_HEADS, HEAD_SIZE)
    gradient_per_head = output_gradient.astype(jnp.float32).reshape(QUERY_ROWS, QUERY_PER_KV, KEY_VALUE_HEADS, HEAD_SIZE)
    key_tiles = keys.astype(jnp.float32).reshape(N_DP, KEYS_PER_SHARD, KEY_VALUE_HEADS, HEAD_SIZE)
    value_tiles = values.astype(jnp.float32).reshape(N_DP, KEYS_PER_SHARD, KEY_VALUE_HEADS, HEAD_SIZE)
    query_at = CONTEXT_KEYS + jnp.arange(QUERY_ROWS, dtype=jnp.int32)
    query_doc = doc_ids[CONTEXT_KEYS:]
    key_at = jnp.arange(KEY_TOTAL, dtype=jnp.int32).reshape(N_DP, KEYS_PER_SHARD)
    key_doc = doc_ids.reshape(N_DP, KEYS_PER_SHARD)
    indices = jnp.arange(N_DP, dtype=jnp.int32)

    def allowed_of(index):
        earlier = key_at[index][None, :] <= query_at[:, None]
        same_doc = key_doc[index][None, :] == query_doc[:, None]
        return (earlier & same_doc)[None, None]

    def scores_of(index):
        return jnp.einsum("qjgd,kgd->gjqk", query_head_rows, key_tiles[index]) * scale_factor

    def block_max(index):
        return jnp.max(jnp.where(allowed_of(index), scores_of(index), NEGATIVE), axis=-1)

    row_max = jnp.max(lax.map(block_max, indices), axis=0)

    def forward_step(totals, index):
        weights = jnp.where(allowed_of(index), jnp.exp(scores_of(index) - row_max[..., None]), 0.0)
        weighted = jnp.einsum("gjqk,kgd->gjqd", settle(weights), value_tiles[index])
        return (totals[0] + weighted, totals[1] + jnp.sum(weights, axis=-1)), index

    empty_output = jnp.zeros((KEY_VALUE_HEADS, QUERY_PER_KV, QUERY_ROWS, HEAD_SIZE), jnp.float32)
    empty_norm = jnp.zeros((KEY_VALUE_HEADS, QUERY_PER_KV, QUERY_ROWS), jnp.float32)
    (summed, norm_sum), unused = lax.scan(forward_step, (empty_output, empty_norm), indices)
    attention = (summed / norm_sum[..., None]).transpose(2, 1, 0, 3).astype(jnp.bfloat16)
    log_norm = row_max + jnp.log(norm_sum)
    row_delta = jnp.sum(gradient_per_head * attention.astype(jnp.float32), axis=-1).transpose(2, 1, 0)

    def backward_step(query_row_count, index):
        probs = jnp.where(allowed_of(index), jnp.exp(scores_of(index) - log_norm[..., None]), 0.0)
        value_grad = jnp.einsum("gjqk,qjgd->kgd", settle(probs), gradient_per_head)
        weight_grad = jnp.einsum("qjgd,kgd->gjqk", gradient_per_head, value_tiles[index])
        score_grad = settle(probs * (weight_grad - row_delta[..., None]))
        q_term = jnp.einsum("gjqk,kgd->qjgd", score_grad, key_tiles[index]) * scale_factor
        key_grad = jnp.einsum("gjqk,qjgd->kgd", score_grad, query_head_rows) * scale_factor
        return query_row_count + settle(q_term), (key_grad, value_grad)

    query_offset = jnp.zeros((QUERY_ROWS, QUERY_PER_KV, KEY_VALUE_HEADS, HEAD_SIZE), jnp.float32)
    query_row_count, (key_gradient_rows, value_gradient_rows) = lax.scan(backward_step, query_offset, indices)
    return (attention.reshape(QUERY_ROWS, QUERY_PER_KV, KEY_VALUE_HEADS * HEAD_SIZE),
            query_row_count.reshape(QUERY_ROWS, QUERY_PER_KV, KEY_VALUE_HEADS * HEAD_SIZE).astype(jnp.bfloat16),
            key_gradient_rows.reshape(KEY_TOTAL, KEY_VALUE_HEADS * HEAD_SIZE).astype(jnp.bfloat16),
            value_gradient_rows.reshape(KEY_TOTAL, KEY_VALUE_HEADS * HEAD_SIZE).astype(jnp.bfloat16))
```

```python
import functools

import jax
import jax.numpy as jnp
from jax import lax
from jax.experimental import pallas as pl
from jax.experimental.pallas import tpu as pltpu
from jax.sharding import PartitionSpec as P

HEAD = 128
DP = 16
QUAD = 4
WINDOW = 10
PAIRS = WINDOW // 2
DOCS = 8
SCALE = HEAD**-0.5
EXP2_SCALE = SCALE * 1.4426950408889634
NEGATIVE = -1e30
QUADS = tuple(tuple(range(QUAD * q, QUAD * q + QUAD)) for q in range(DP // QUAD))

F32 = jnp.float32
BF16 = jnp.bfloat16
NT = (((1,), (1,)), ((), ()))
NN = (((1,), (0,)), ((), ()))
TN = (((0,), (0,)), ((), ()))


def dot(lhs, rhs, dims):
    return lax.dot_general(lhs, rhs, dims, preferred_element_type=F32)


def place_pattern(rows):
    at = lax.broadcasted_iota(jnp.int32, (rows, 128), 0)
    srv, rest = at // 80, at % 80
    shard, rest = rest // 40, rest % 40
    return 640 * shard + 80 * (rest // 20) + 20 * srv + rest % 20


def fold8(block, op):
    rows, cols = block.shape
    return op(block.reshape(rows // 8, 8, cols), axis=0)


def forward_kernel(info, starts, qg, kv, e_ref, o_ref, stats_ref, s_ref, m_ref, l_ref):
    first, last, place, query_at = info[0], info[1], info[2], info[3]
    tiles, cols, _ = qg.shape
    keys = kv.shape[0] * kv.shape[2]
    pattern = place + place_pattern(keys)
    pattern = jnp.concatenate([pattern] * (cols // 128), axis=1)
    lane = lax.broadcasted_iota(jnp.int32, (1, cols), 1)
    m_ref[...] = jnp.full(m_ref.shape, NEGATIVE, F32)
    l_ref[...] = jnp.zeros(l_ref.shape, F32)
    o_ref[...] = jnp.zeros(o_ref.shape, F32)
    query_places, doc_starts = [], []
    for tile in range(tiles):
        query_place = query_at + (cols // 2) * tile + lane // 2
        doc_start = jnp.zeros_like(query_place)
        for doc in range(DOCS):
            doc_start = jnp.where(
                starts[doc] <= query_place, jnp.maximum(doc_start, starts[doc]), doc_start
            )
        query_places.append(query_place)
        doc_starts.append(doc_start)

    def scores(t, carry):
        k = kv[:, t, :, :HEAD].reshape(keys, HEAD)
        key_place = pattern + 1280 * t
        for tile in range(tiles):
            span = pl.ds(tile * cols, cols)
            s = dot(k, qg[tile, :, :HEAD], NT)
            allowed = (key_place >= doc_starts[tile]) & (key_place <= query_places[tile])
            s = jnp.where(allowed, s, NEGATIVE)
            s_ref[t, :, span] = s
            m_ref[tile] = jnp.maximum(m_ref[tile], fold8(s, jnp.max))
        return carry

    lax.fori_loop(first, last, scores, 0)
    tops = [jnp.max(m_ref[tile], axis=0, keepdims=True) for tile in range(tiles)]

    def weigh(t, carry):
        v = kv[:, t, :, HEAD:].reshape(keys, HEAD)
        for tile in range(tiles):
            span = pl.ds(tile * cols, cols)
            e = jnp.exp2((s_ref[t, :, span] - tops[tile]) * EXP2_SCALE)
            l_ref[tile] += fold8(e, jnp.sum)
            e = e.astype(BF16)
            e_ref[t, :, span] = e
            o_ref[tile] += dot(v, e, TN)
        return carry

    lax.fori_loop(first, last, weigh, 0)
    stats_ref[...] = jnp.zeros(stats_ref.shape, F32)
    for tile in range(tiles):
        gradient = qg[tile, :, HEAD:].astype(F32).T
        stats_ref[tile : tile + 1, :] = tops[tile]
        stats_ref[tiles + tile : tiles + tile + 1, :] = jnp.sum(
            l_ref[tile], axis=0, keepdims=True
        )
        stats_ref[2 * tiles + tile : 2 * tiles + tile + 1, :] = jnp.sum(
            gradient * o_ref[tile], axis=0, keepdims=True
        )


def backward_kernel(info, qg, kv, e_ref, o_ref, own, stats, oq_ref, dkv_ref, dq_ref):
    first, last = info[0], info[1]
    tiles, cols, _ = qg.shape
    keys = kv.shape[0] * kv.shape[2]
    dkv_ref[...] = jnp.zeros(dkv_ref.shape, BF16)
    dq_ref[...] = jnp.zeros(dq_ref.shape, F32)
    shares, deltas = [], []
    for tile in range(tiles):
        row = lambda ref, kind: ref[kind * tiles + tile : kind * tiles + tile + 1, :]
        parts = [stats.at[part] for part in range(stats.shape[0])]
        top = functools.reduce(jnp.maximum, [row(p, 0) for p in parts])
        weights = [jnp.exp2((row(p, 0) - top) * EXP2_SCALE) for p in parts]
        norm = sum(w * row(p, 1) for w, p in zip(weights, parts))
        deltas.append(sum(w * row(p, 2) for w, p in zip(weights, parts)) / norm)
        shares.append(jnp.exp2((row(own, 0) - top) * EXP2_SCALE) / norm)

    def grads(t, carry):
        k = kv[:, t, :, :HEAD].reshape(keys, HEAD)
        v = kv[:, t, :, HEAD:].reshape(keys, HEAD)
        dk = jnp.zeros((keys, HEAD), F32)
        dv = jnp.zeros((keys, HEAD), F32)
        for tile in range(tiles):
            q, gradient = qg[tile, :, :HEAD], qg[tile, :, HEAD:]
            p = e_ref[t, :, pl.ds(tile * cols, cols)].astype(F32) * shares[tile]
            ds = (p * (dot(v, gradient, NT) - deltas[tile])).astype(BF16)
            dv += dot(p.astype(BF16), gradient, NN)
            dk += dot(ds, q, NN)
            dq_ref[tile] += dot(k, ds, TN)
        dk = (dk * SCALE).astype(BF16).reshape(kv.shape[0], kv.shape[2], HEAD)
        dv = dv.astype(BF16).reshape(kv.shape[0], kv.shape[2], HEAD)
        dkv_ref[:, t, :, :HEAD] = dk
        dkv_ref[:, t, :, HEAD:] = dv
        return carry

    lax.fori_loop(first, last, grads, 0)
    for tile in range(tiles):
        oq_ref[tile, :, :HEAD] = (o_ref[tile] * shares[tile]).T.astype(BF16)
        oq_ref[tile, :, HEAD:] = (dq_ref[tile] * SCALE).T.astype(BF16)


def exchange(block, axis, groups=None):
    return lax.all_to_all(block, axis, 0, 0, tiled=True, axis_index_groups=groups)


def spread(block, count):
    return jnp.broadcast_to(block[None], (count, *block.shape))


def local(queries, keys, values, output_gradient, doc_ids):
    rows = queries.shape[0] * queries.shape[1]
    dp, srv = lax.axis_index("dp"), lax.axis_index("srv")
    quad, member = dp // QUAD, dp % QUAD
    heads, srvs = 8, 4
    shard_rows = keys.shape[0] // srvs
    vmem = pl.BlockSpec(memory_space=pltpu.VMEM)
    smem = pl.BlockSpec(memory_space=pltpu.SMEM)

    mine = lambda x: lax.dynamic_slice_in_dim(x, srv * shard_rows, shard_rows, 0).reshape(
        shard_rows, heads, HEAD
    )
    kv = jnp.concatenate([mine(keys), mine(values)], axis=2).transpose(1, 0, 2)
    kv = exchange(kv, "head")
    kv = kv.reshape(QUAD, heads // QUAD * shard_rows, 2 * HEAD)
    count = jnp.sum(
        (doc_ids[:, None] == jnp.arange(DOCS, dtype=jnp.int32)[None, :]).astype(jnp.int32), axis=0
    )
    count = jnp.concatenate([count // 128, count % 128]).astype(BF16)
    extra = jnp.zeros((QUAD, 8, 2 * HEAD), BF16).at[:, 0, : 2 * DOCS].set(count[None])
    piece = kv.shape[1]
    kv = spread(jnp.concatenate([kv, extra], axis=1), DP // QUAD)
    kv = exchange(kv.reshape(DP, piece + 8, 2 * HEAD), "dp")
    count = jnp.sum(kv[:, piece, : 2 * DOCS].astype(F32), axis=0).astype(jnp.int32)
    count = count[:DOCS] * 128 + count[DOCS:]
    doc = jnp.arange(DOCS, dtype=jnp.int32)
    starts = jnp.sum(jnp.where(doc[None, :] < doc[:, None], count[None, :], 0), axis=1)
    window = jnp.minimum(4 + quad, DP - WINDOW)
    kv = lax.dynamic_slice(kv, (window, 0, 0), (WINDOW, piece, 2 * HEAD))
    kv = exchange(spread(kv, srvs), "srv", None)
    kv = kv.reshape(srvs, PAIRS, 2 * piece, 2 * HEAD)

    qg = jnp.concatenate(
        [queries.reshape(rows, HEAD), output_gradient.reshape(rows, HEAD)], axis=1
    )
    qg = exchange(spread(qg, QUAD), "dp", QUADS)
    qg = qg.reshape(QUAD, rows, 2 * HEAD)

    query_at = 8192 + 512 * quad
    doc_start = jnp.max(jnp.where(starts <= query_at, starts, 0))
    first = jnp.maximum(doc_start // 640 - window, 0) // 2
    last = jnp.minimum(((query_at + 511) // 640 - window) // 2 + 1, PAIRS)
    info = jnp.stack([first, last, 640 * window + 160 * member, query_at]).astype(jnp.int32)

    key_block = srvs * 2 * piece
    params = pltpu.CompilerParams(vmem_limit_bytes=40 * 1024 * 1024)
    e, o, stats = pl.pallas_call(
        forward_kernel,
        out_shape=(
            jax.ShapeDtypeStruct((PAIRS, key_block, QUAD * rows), BF16),
            jax.ShapeDtypeStruct((QUAD, HEAD, rows), F32),
            jax.ShapeDtypeStruct((16, rows), F32),
        ),
        in_specs=[smem, smem, vmem, vmem],
        out_specs=(vmem, vmem, vmem),
        scratch_shapes=[
            pltpu.VMEM((PAIRS, key_block, QUAD * rows), F32),
            pltpu.VMEM((QUAD, 8, rows), F32),
            pltpu.VMEM((QUAD, 8, rows), F32),
        ],
        compiler_params=params,
        name="forward",
    )(info, starts, qg, kv)
    all_stats = exchange(spread(stats, QUAD).reshape(QUAD * 16, rows), "dp", QUADS)
    all_stats = all_stats.reshape(QUAD, 16, rows)
    oq, dkv = pl.pallas_call(
        backward_kernel,
        out_shape=(
            jax.ShapeDtypeStruct((QUAD, rows, 2 * HEAD), BF16),
            jax.ShapeDtypeStruct(kv.shape, BF16),
        ),
        in_specs=[smem, vmem, vmem, vmem, vmem, vmem, vmem],
        out_specs=(vmem, vmem),
        scratch_shapes=[pltpu.VMEM((QUAD, HEAD, rows), F32)],
        compiler_params=params,
        name="backward",
    )(info, qg, kv, e, o, stats, all_stats)

    total = lambda x: jnp.sum(x.astype(F32), axis=0).astype(BF16)
    dkv = exchange(dkv.reshape(srvs, WINDOW, piece, 2 * HEAD), "srv")
    dkv = lax.dynamic_update_slice(
        jnp.zeros((DP, piece, 2 * HEAD), BF16), total(dkv), (window, 0, 0)
    )
    dkv = exchange(dkv, "dp")
    dkv = total(dkv.reshape(DP // QUAD, QUAD, piece, 2 * HEAD))
    dkv = exchange(dkv.reshape(heads, shard_rows, 2 * HEAD), "head")
    dkv = dkv.transpose(1, 0, 2)
    k_grad = dkv[:, :, :HEAD].reshape(shard_rows, heads * HEAD)
    v_grad = dkv[:, :, HEAD:].reshape(shard_rows, heads * HEAD)

    oq = total(exchange(oq, "dp", QUADS))
    attention = oq[:, :HEAD].reshape(queries.shape)
    q_grad = oq[:, HEAD:].reshape(queries.shape)
    return attention, q_grad, k_grad, v_grad


def solution(mesh):
    placed = (
        P("dp", "srv", "head"),
        P(("dp", "head"), None),
        P(("dp", "head"), None),
        P("dp", "srv", "head"),
        P("dp"),
    )
    return jax.shard_map(
        local,
        mesh=mesh,
        in_specs=placed,
        out_specs=(
            P("dp", "srv", "head"),
            P("dp", "srv", "head"),
            P(("dp", "head", "srv"), None),
            P(("dp", "head", "srv"), None),
        ),
        check_vma=False,
    )
```

```python
import functools

import jax
import jax.numpy as jnp
from jax import lax
from jax.experimental import pallas as pl
from jax.experimental.pallas import tpu as pltpu
from jax.sharding import PartitionSpec as P

HEAD = 128
DP = 16
QUAD = 4
BLOCKS = 3
SHARD = 640
CONTEXT = 8192
DOCS = 8
SCALE = HEAD**-0.5
EXP2_SCALE = SCALE * 1.4426950408889634
NEGATIVE = -1e30
NEAR = tuple(tuple(range(QUAD * q, QUAD * q + QUAD)) for q in range(DP // QUAD))
FAR = tuple(tuple(range(m, DP, QUAD)) for m in range(QUAD))

F32 = jnp.float32
BF16 = jnp.bfloat16
NT = (((1,), (1,)), ((), ()))
NN = (((1,), (0,)), ((), ()))
TN = (((0,), (0,)), ((), ()))


def dot(lhs, rhs, dims):
    return lax.dot_general(lhs, rhs, dims, preferred_element_type=F32)


def fold8(block, op):
    rows, cols = block.shape
    return op(block.reshape(rows // 8, 8, cols), axis=0)


def member_of(member, turn):
    return lax.rem(member - turn + QUAD, QUAD)


def forward_kernel(
    info, q0, q1, q2, q3, kv, e_ref, o_ref, stats_ref, active, s_ref, m_ref, l_ref
):
    quad, member = info[0], info[1]
    qs = (q0, q1, q2, q3)
    cols = o_ref.shape[2]
    srvs, _, part, _ = kv.shape
    keys = srvs * part
    query_at = CONTEXT + 2 * cols * quad

    count = sum(jnp.sum(q[cols:, :].astype(F32), axis=0, keepdims=True) for q in qs)
    lanes = lax.broadcasted_iota(jnp.int32, count.shape, 1)
    starts = []
    for doc in range(DOCS):
        high = jnp.sum(jnp.where(lanes < doc, count, 0.0)) * 64.0
        low = jnp.sum(jnp.where((lanes >= DOCS) & (lanes < DOCS + doc), count, 0.0))
        starts.append((high + low).astype(jnp.int32))
    reach = jnp.int32(0)
    for start in starts:
        reach = jnp.where(start <= query_at, jnp.maximum(reach, start), reach)
    first, last = jnp.int32(0), jnp.int32(0)
    for block in range(BLOCKS):
        shard = SHARD * (QUAD * (block + 1) + member)
        first += (shard + SHARD <= reach).astype(jnp.int32)
        last += (shard < query_at + 2 * cols).astype(jnp.int32)
    active[0] = first
    active[1] = last

    at = lax.broadcasted_iota(jnp.int32, (keys, 128), 0)
    rest = at % part
    pattern = 80 * (rest // 20) + 20 * (at // part) + rest % 20 + SHARD * (QUAD + member)
    pattern = jnp.concatenate([pattern] * (cols // 128), axis=1)
    lane = lax.broadcasted_iota(jnp.int32, (1, cols), 1)
    m_ref[...] = jnp.full(m_ref.shape, NEGATIVE, F32)
    l_ref[...] = jnp.zeros(l_ref.shape, F32)
    o_ref[...] = jnp.zeros(o_ref.shape, F32)
    query_places, doc_starts = [], []
    for turn in range(QUAD):
        query_place = query_at + (cols // 2) * member_of(member, turn) + lane // 2
        doc_start = jnp.zeros_like(query_place)
        for start in starts:
            doc_start = jnp.where(start <= query_place, jnp.maximum(doc_start, start), doc_start)
        query_places.append(query_place)
        doc_starts.append(doc_start)

    def scores(t, carry):
        k = kv[:, t, :, :HEAD].reshape(keys, HEAD)
        key_place = pattern + QUAD * SHARD * t
        for turn in range(QUAD):
            span = pl.ds(turn * cols, cols)
            s = dot(k, qs[turn][:cols, :HEAD], NT)
            allowed = (key_place >= doc_starts[turn]) & (key_place <= query_places[turn])
            s = jnp.where(allowed, s, NEGATIVE)
            s_ref[t, :, span] = s
            m_ref[turn] = jnp.maximum(m_ref[turn], fold8(s, jnp.max))
        return carry

    lax.fori_loop(first, last, scores, 0)
    tops = [jnp.max(m_ref[turn], axis=0, keepdims=True) for turn in range(QUAD)]

    def weigh(t, carry):
        v = kv[:, t, :, HEAD:].reshape(keys, HEAD)
        for turn in range(QUAD):
            span = pl.ds(turn * cols, cols)
            e = jnp.exp2((s_ref[t, :, span] - tops[turn]) * EXP2_SCALE)
            l_ref[turn] += fold8(e, jnp.sum)
            e = e.astype(BF16)
            e_ref[t, :, span] = e
            o_ref[turn] += dot(v, e, TN)
        return carry

    lax.fori_loop(first, last, weigh, 0)
    for turn in range(QUAD):
        tile = member_of(member, turn)
        gradient = qs[turn][:cols, HEAD:].astype(F32).T
        norm = jnp.sum(l_ref[turn], axis=0, keepdims=True)
        delta = jnp.sum(gradient * o_ref[turn], axis=0, keepdims=True)
        for copy in range(QUAD):
            stats_ref[copy, pl.ds(tile, 1), :] = tops[turn]
            stats_ref[copy, pl.ds(QUAD + tile, 1), :] = norm
            stats_ref[copy, pl.ds(2 * QUAD + tile, 1), :] = delta
            stats_ref[copy, pl.ds(3 * QUAD + tile, 1), :] = jnp.zeros_like(norm)


def backward_kernel(
    info, active, q0, q1, q2, q3, kv, e_ref, o_ref, stats, oq0, oq1, oq2, oq3, dkv_ref, dq_ref
):
    member = info[1]
    first, last = active[0], active[1]
    qs, oqs = (q0, q1, q2, q3), (oq0, oq1, oq2, oq3)
    cols = o_ref.shape[2]
    srvs, _, part, _ = kv.shape
    keys = srvs * part
    dq_ref[...] = jnp.zeros(dq_ref.shape, F32)
    shares, deltas = [], []
    for turn in range(QUAD):
        tile = member_of(member, turn)
        row = lambda who, kind: stats[who, pl.ds(kind * QUAD + tile, 1), :]
        top = functools.reduce(jnp.maximum, [row(who, 0) for who in range(QUAD)])
        weights = [jnp.exp2((row(who, 0) - top) * EXP2_SCALE) for who in range(QUAD)]
        norm = sum(weights[who] * row(who, 1) for who in range(QUAD))
        deltas.append(sum(weights[who] * row(who, 2) for who in range(QUAD)) / norm)
        shares.append(jnp.exp2((row(member, 0) - top) * EXP2_SCALE) / norm)

    def clear(t, carry):
        dkv_ref[:, t] = jnp.zeros((srvs, part, 2 * HEAD), BF16)
        return carry

    lax.fori_loop(0, first, clear, 0)
    lax.fori_loop(last, BLOCKS, clear, 0)

    def grads(t, carry):
        k = kv[:, t, :, :HEAD].reshape(keys, HEAD)
        v = kv[:, t, :, HEAD:].reshape(keys, HEAD)
        dk = jnp.zeros((keys, HEAD), F32)
        dv = jnp.zeros((keys, HEAD), F32)
        for turn in range(QUAD):
            q, gradient = qs[turn][:cols, :HEAD], qs[turn][:cols, HEAD:]
            p = e_ref[t, :, pl.ds(turn * cols, cols)].astype(F32) * shares[turn]
            ds = (p * (dot(v, gradient, NT) - deltas[turn])).astype(BF16)
            dv += dot(p.astype(BF16), gradient, NN)
            dk += dot(ds, q, NN)
            dq_ref[turn] += dot(k, ds, TN)
        dkv_ref[:, t, :, :HEAD] = (dk * SCALE).astype(BF16).reshape(srvs, part, HEAD)
        dkv_ref[:, t, :, HEAD:] = dv.astype(BF16).reshape(srvs, part, HEAD)
        return carry

    lax.fori_loop(first, last, grads, 0)
    for turn in range(QUAD):
        oqs[turn][:, :HEAD] = (o_ref[turn] * shares[turn]).T.astype(BF16)
        oqs[turn][:, HEAD:] = (dq_ref[turn] * SCALE).T.astype(BF16)


def exchange(block, axis, groups=None):
    return lax.all_to_all(block, axis, 0, 0, tiled=True, axis_index_groups=groups)


def rotate(block, turn):
    pairs = [(q[i], q[(i + turn) % QUAD]) for q in NEAR for i in range(QUAD)]
    return lax.ppermute(block, "dp", pairs)


def local(queries, keys, values, output_gradient, doc_ids):
    rows = queries.shape[0] * queries.shape[1]
    heads, srvs = 8, 4
    dp, srv = lax.axis_index("dp"), lax.axis_index("srv")
    info = jnp.stack([dp // QUAD, dp % QUAD]).astype(jnp.int32)
    shard_rows = keys.shape[0] // srvs
    part = heads * shard_rows
    vmem = pl.BlockSpec(memory_space=pltpu.VMEM)
    smem = pl.BlockSpec(memory_space=pltpu.SMEM)

    mine = lambda x: lax.dynamic_slice_in_dim(x, srv * shard_rows, shard_rows, 0).reshape(
        shard_rows, heads, HEAD
    )
    kv = jnp.concatenate([mine(keys), mine(values)], axis=2).transpose(1, 0, 2)
    kv = exchange(kv, "head").reshape(part, 2 * HEAD)
    count = jnp.sum(
        (doc_ids[:, None] == jnp.arange(DOCS, dtype=jnp.int32)[None, :]).astype(jnp.int32), axis=0
    )
    count = jnp.concatenate([count // 64, count % 64]).astype(BF16)
    count = jnp.pad(count[None], ((0, 7), (0, 2 * HEAD - 2 * DOCS)))
    kv = jnp.concatenate([kv, count], axis=0)
    kv = lax.all_gather(kv, "dp", axis=0, axis_index_groups=FAR)
    count = jnp.sum(kv[:, part:].astype(F32), axis=0).astype(BF16)
    kv = jnp.broadcast_to(kv[None, 1:, :part], (srvs, BLOCKS, part, 2 * HEAD))
    kv = exchange(kv, "srv").reshape(srvs, BLOCKS, part, 2 * HEAD)

    qg = jnp.concatenate(
        [queries.reshape(rows, HEAD), output_gradient.reshape(rows, HEAD)], axis=1
    )
    qg = jnp.concatenate([qg, count], axis=0)
    qs = [qg] + [rotate(qg, turn) for turn in range(1, QUAD)]

    key_block = srvs * part
    params = pltpu.CompilerParams(vmem_limit_bytes=40 * 1024 * 1024)
    e, o, stats, active = pl.pallas_call(
        forward_kernel,
        out_shape=(
            jax.ShapeDtypeStruct((BLOCKS, key_block, QUAD * rows), BF16),
            jax.ShapeDtypeStruct((QUAD, HEAD, rows), F32),
            jax.ShapeDtypeStruct((QUAD, 4 * QUAD, rows), F32),
            jax.ShapeDtypeStruct((2,), jnp.int32),
        ),
        in_specs=[smem] + [vmem] * 5,
        out_specs=(vmem, vmem, vmem, smem),
        scratch_shapes=[
            pltpu.VMEM((BLOCKS, key_block, QUAD * rows), F32),
            pltpu.VMEM((QUAD, 8, rows), F32),
            pltpu.VMEM((QUAD, 8, rows), F32),
        ],
        compiler_params=params,
        name="forward",
    )(info, *qs, kv)
    stats = exchange(stats.reshape(QUAD * 4 * QUAD, rows), "dp", NEAR)
    stats = stats.reshape(QUAD, 4 * QUAD, rows)
    *oqs, dkv = pl.pallas_call(
        backward_kernel,
        out_shape=(
            *[jax.ShapeDtypeStruct((rows, 2 * HEAD), BF16)] * QUAD,
            jax.ShapeDtypeStruct(kv.shape, BF16),
        ),
        in_specs=[smem, smem] + [vmem] * 8,
        out_specs=(vmem,) * 5,
        scratch_shapes=[pltpu.VMEM((QUAD, HEAD, rows), F32)],
        compiler_params=params,
        name="backward",
    )(info, active, *qs, kv, e, o, stats)

    oqs = [oqs[0]] + [rotate(oqs[turn], -turn) for turn in range(1, QUAD)]
    total = lambda x: jnp.sum(x.astype(F32), axis=0).astype(BF16)
    dkv = exchange(dkv, "srv")
    dkv, oqs = lax.optimization_barrier((dkv, oqs))
    dkv = total(dkv)
    dkv = jnp.concatenate([jnp.zeros_like(dkv[:1]), dkv], axis=0)
    dkv = total(exchange(dkv, "dp", FAR))
    dkv = exchange(dkv.reshape(heads, shard_rows, 2 * HEAD), "head")
    dkv = dkv.transpose(1, 0, 2)
    k_grad = dkv[:, :, :HEAD].reshape(shard_rows, heads * HEAD)
    v_grad = dkv[:, :, HEAD:].reshape(shard_rows, heads * HEAD)

    oq = sum(x.astype(F32) for x in oqs).astype(BF16)
    attention = oq[:, :HEAD].reshape(queries.shape)
    q_grad = oq[:, HEAD:].reshape(queries.shape)
    return attention, q_grad, k_grad, v_grad


def solution(mesh):
    placed = (
        P("dp", "srv", "head"),
        P(("dp", "head"), None),
        P(("dp", "head"), None),
        P("dp", "srv", "head"),
        P("dp"),
    )
    return jax.shard_map(
        local,
        mesh=mesh,
        in_specs=placed,
        out_specs=(
            P("dp", "srv", "head"),
            P("dp", "srv", "head"),
            P(("dp", "head", "srv"), None),
            P(("dp", "head", "srv"), None),
        ),
        check_vma=False,
    )
```

```python
import functools

import jax
import jax.numpy as jnp
from jax import lax
from jax.experimental import pallas as pl
from jax.experimental.pallas import tpu as pltpu
from jax.sharding import PartitionSpec as P

HEAD = 128
DP = 16
QUAD = 4
BLOCKS = 3
SHARD = 640
CONTEXT = 8192
DOCS = 8
GROUPS = 8
SRVS = 4
PIECE = SHARD // GROUPS // SRVS
SCALE = HEAD**-0.5
EXP2_SCALE = SCALE * 1.4426950408889634
NEGATIVE = -1e30
NEAR = tuple(tuple(range(QUAD * q, QUAD * q + QUAD)) for q in range(DP // QUAD))
FAR = tuple(tuple(range(m, DP, QUAD)) for m in range(QUAD))

F32 = jnp.float32
BF16 = jnp.bfloat16
NT = (((1,), (1,)), ((), ()))
NN = (((1,), (0,)), ((), ()))


def dot(lhs, rhs, dims):
    return lax.dot_general(lhs, rhs, dims, preferred_element_type=F32)


def flip(block):
    size = block.shape[1]
    rows = lax.broadcasted_iota(jnp.int32, (size, size), 0)
    columns = lax.broadcasted_iota(jnp.int32, (size, size), 1)
    return dot((rows == columns).astype(BF16), block, NT)


def fold8(block, op):
    rows, cols = block.shape
    return op(block.reshape(rows // 8, 8, cols), axis=0)


def member_of(member, turn):
    return lax.rem(member - turn + QUAD, QUAD)


def fetch(sources, targets, sems):
    copies = [
        pltpu.make_async_copy(source, target, sems.at[i])
        for i, (source, target) in enumerate(zip(sources, targets))
    ]
    for copy in copies:
        copy.start()
    return copies


def pack_kernel(
    docs_in, keys_in, values_in, out_ref, docs, keys, values, k_ref, v_ref, f_ref, sems
):
    srv = lax.axis_index("srv")
    for copy in fetch((docs_in, keys_in, values_in), (docs, keys, values), sems):
        copy.wait()
    k_ref[...] = keys[...].astype(F32)
    v_ref[...] = values[...].astype(F32)

    def mine(ref):
        piece = ref[:PIECE, :]
        for part in range(1, SRVS):
            other = ref[PIECE * part : PIECE * (part + 1), :]
            piece = jnp.where(srv == part, other, piece)
        return piece

    k, v = mine(k_ref), mine(v_ref)
    for group in range(GROUPS):
        span = slice(PIECE * group, PIECE * (group + 1))
        columns = slice(HEAD * group, HEAD * (group + 1))
        f_ref[span, :HEAD] = k[:, columns]
        f_ref[span, HEAD:] = v[:, columns]
    lanes = lax.broadcasted_iota(jnp.int32, (8, 2 * HEAD), 1)
    row = jnp.zeros((8, 2 * HEAD), F32)
    for doc in range(DOCS):
        count = jnp.sum(jnp.where(docs[...] == doc, 1.0, 0.0), axis=1, keepdims=True)
        count = jnp.sum(count, axis=0, keepdims=True).astype(jnp.int32)
        row = jnp.where(lanes == doc, (count >> 6).astype(F32), row)
        row = jnp.where(lanes == DOCS + doc, (count & 63).astype(F32), row)
    first = lax.broadcasted_iota(jnp.int32, (8, 2 * HEAD), 0) == 0
    f_ref[PIECE * GROUPS :, :] = jnp.where(first, row, 0.0)
    out_ref[...] = f_ref[...].astype(BF16)


def fan_kernel(gathered, queries, gradient, out_ref, qg_ref, f_ref, slab_ref, sems):
    rows = queries.shape[0]
    targets = (qg_ref.at[pl.ds(0, rows), pl.ds(0, HEAD)], qg_ref.at[pl.ds(0, rows), pl.ds(HEAD, HEAD)])
    copies = fetch((queries, gradient), targets, sems)
    for quad in range(QUAD):
        f_ref[quad] = gathered[quad].astype(F32)
    for group in range(GROUPS):
        for block in range(BLOCKS):
            slab_ref[group, PIECE * block : PIECE * (block + 1), :] = f_ref[
                block + 1, PIECE * group : PIECE * (group + 1), :
            ]
        slab = slab_ref[group].astype(BF16)
        for srv in range(SRVS):
            out_ref[group, srv] = slab
    count = sum(f_ref[quad, PIECE * GROUPS :, :] for quad in range(QUAD))
    qg_ref[rows:, :] = count.astype(BF16)
    for copy in copies:
        copy.wait()


def fold_kernel(parts, out_ref, slab_ref, f_ref):
    for group in range(GROUPS):
        slab_ref[group] = sum(parts[group, srv].astype(F32) for srv in range(SRVS))
        for block in range(BLOCKS):
            f_ref[block, PIECE * group : PIECE * (group + 1), :] = slab_ref[
                group, PIECE * block : PIECE * (block + 1), :
            ]
    out_ref[0] = jnp.zeros(out_ref.shape[1:], BF16)
    for block in range(BLOCKS):
        out_ref[block + 1] = f_ref[block].astype(BF16)


def finish_kernel(parts, k_ref, v_ref, f_ref):
    f_ref[...] = sum(parts[quad].astype(F32) for quad in range(QUAD))
    for group in range(GROUPS):
        span = slice(PIECE * group, PIECE * (group + 1))
        columns = slice(HEAD * group, HEAD * (group + 1))
        k_ref[:, columns] = f_ref[span, :HEAD].astype(BF16)
        v_ref[:, columns] = f_ref[span, HEAD:].astype(BF16)


def forward_kernel(
    qg, slabs, e_ref, o_ref, stats_ref, active, kv, s_ref, m_ref, l_ref, slab_ref, f_ref
):
    dp = lax.axis_index("dp")
    quad, member = dp // QUAD, dp % QUAD
    qs = [qg.at[member_of(member, turn)] for turn in range(QUAD)]
    cols = o_ref.shape[2]
    keys = kv.shape[1]
    query_at = CONTEXT + 2 * cols * quad

    count = sum(jnp.sum(qg[who, cols:, :].astype(F32), axis=0, keepdims=True) for who in range(QUAD))
    lanes = lax.broadcasted_iota(jnp.int32, count.shape, 1)
    starts = []
    for doc in range(DOCS):
        high = jnp.sum(jnp.where(lanes < doc, count, 0.0)) * 64.0
        low = jnp.sum(jnp.where((lanes >= DOCS) & (lanes < DOCS + doc), count, 0.0))
        starts.append((high + low).astype(jnp.int32))
    reach = jnp.int32(0)
    for start in starts:
        reach = jnp.where(start <= query_at, jnp.maximum(reach, start), reach)
    first, last = jnp.int32(0), jnp.int32(0)
    for block in range(BLOCKS):
        shard = SHARD * (QUAD * (block + 1) + member)
        first += (shard + SHARD <= reach).astype(jnp.int32)
        last += (shard < query_at + 2 * cols).astype(jnp.int32)
    active[0] = first
    active[1] = last

    for group in range(GROUPS):
        for srv in range(SRVS):
            slab_ref[group, srv] = slabs[group, srv].astype(F32)
            at = PIECE * (SRVS * group + srv)
            for block in range(BLOCKS):
                f_ref[block, at : at + PIECE, :] = slab_ref[
                    group, srv, PIECE * block : PIECE * (block + 1), :
                ]
    for block in range(BLOCKS):
        kv[block] = f_ref[block].astype(BF16)

    pattern = lax.broadcasted_iota(jnp.int32, (keys, cols), 0) + SHARD * (QUAD + member)
    lane = lax.broadcasted_iota(jnp.int32, (1, cols), 1)
    m_ref[...] = jnp.full(m_ref.shape, NEGATIVE, F32)
    l_ref[...] = jnp.zeros(l_ref.shape, F32)
    o_ref[...] = jnp.zeros(o_ref.shape, F32)
    query_places, doc_starts = [], []
    for turn in range(QUAD):
        query_place = query_at + (cols // 2) * member_of(member, turn) + lane // 2
        doc_start = jnp.zeros_like(query_place)
        for start in starts:
            doc_start = jnp.where(start <= query_place, jnp.maximum(doc_start, start), doc_start)
        query_places.append(query_place)
        doc_starts.append(doc_start)

    def scores(t, carry):
        k = kv[t, :, :HEAD]
        key_place = pattern + QUAD * SHARD * t
        for turn in range(QUAD):
            span = pl.ds(turn * cols, cols)
            s = dot(k, qs[turn][:cols, :HEAD], NT)
            allowed = (key_place >= doc_starts[turn]) & (key_place <= query_places[turn])
            s = jnp.where(allowed, s, NEGATIVE)
            s_ref[t, :, span] = s
            m_ref[turn] = jnp.maximum(m_ref[turn], fold8(s, jnp.max))
        return carry

    lax.fori_loop(first, last, scores, 0)
    tops = [jnp.max(m_ref[turn], axis=0, keepdims=True) for turn in range(QUAD)]

    def weigh(t, carry):
        v = flip(kv[t, :, HEAD:]).astype(BF16)
        for turn in range(QUAD):
            span = pl.ds(turn * cols, cols)
            e = jnp.exp2((s_ref[t, :, span] - tops[turn]) * EXP2_SCALE)
            l_ref[turn] += fold8(e, jnp.sum)
            e = e.astype(BF16)
            e_ref[t, :, span] = e
            o_ref[turn] += dot(v, e, NN)
        return carry

    lax.fori_loop(first, last, weigh, 0)
    for turn in range(QUAD):
        tile = member_of(member, turn)
        gradient = flip(qs[turn][:cols, HEAD:])
        norm = jnp.sum(l_ref[turn], axis=0, keepdims=True)
        delta = jnp.sum(gradient * o_ref[turn], axis=0, keepdims=True)
        for copy in range(QUAD):
            stats_ref[copy, pl.ds(tile, 1), :] = tops[turn]
            stats_ref[copy, pl.ds(QUAD + tile, 1), :] = norm
            stats_ref[copy, pl.ds(2 * QUAD + tile, 1), :] = delta
            stats_ref[copy, pl.ds(3 * QUAD + tile, 1), :] = jnp.zeros_like(norm)


def backward_kernel(
    active, qg, kv, e_ref, o_ref, stats, oq0, oq1, oq2, oq3, dkv_ref, dq_ref, f_ref, slab_ref
):
    member = lax.axis_index("dp") % QUAD
    first, last = active[0], active[1]
    qs = [qg.at[member_of(member, turn)] for turn in range(QUAD)]
    oqs = (oq0, oq1, oq2, oq3)
    cols = o_ref.shape[2]
    keys = kv.shape[1]
    dq_ref[...] = jnp.zeros(dq_ref.shape, F32)
    shares, deltas = [], []
    for turn in range(QUAD):
        tile = member_of(member, turn)
        row = lambda who, kind: stats[who, pl.ds(kind * QUAD + tile, 1), :]
        top = functools.reduce(jnp.maximum, [row(who, 0) for who in range(QUAD)])
        weights = [jnp.exp2((row(who, 0) - top) * EXP2_SCALE) for who in range(QUAD)]
        norm = sum(weights[who] * row(who, 1) for who in range(QUAD))
        deltas.append(sum(weights[who] * row(who, 2) for who in range(QUAD)) / norm)
        shares.append(jnp.exp2((row(member, 0) - top) * EXP2_SCALE) / norm)

    def clear(t, carry):
        f_ref[t] = jnp.zeros((keys, 2 * HEAD), F32)
        return carry

    lax.fori_loop(0, first, clear, 0)
    lax.fori_loop(last, BLOCKS, clear, 0)

    def grads(t, carry):
        k = kv[t, :, :HEAD]
        v = kv[t, :, HEAD:]
        kt = flip(k).astype(BF16)
        dk = jnp.zeros((keys, HEAD), F32)
        dv = jnp.zeros((keys, HEAD), F32)
        for turn in range(QUAD):
            q, gradient = qs[turn][:cols, :HEAD], qs[turn][:cols, HEAD:]
            p = e_ref[t, :, pl.ds(turn * cols, cols)].astype(F32) * shares[turn]
            ds = (p * (dot(v, gradient, NT) - deltas[turn])).astype(BF16)
            dv += dot(p.astype(BF16), gradient, NN)
            dk += dot(ds, q, NN)
            dq_ref[turn] += dot(kt, ds, NN)
        f_ref[t, :, :HEAD] = dk * SCALE
        f_ref[t, :, HEAD:] = dv
        return carry

    lax.fori_loop(first, last, grads, 0)
    for turn in range(QUAD):
        oqs[turn][:, :HEAD] = flip((o_ref[turn] * shares[turn]).astype(BF16)).astype(BF16)
        oqs[turn][:, HEAD:] = flip((dq_ref[turn] * SCALE).astype(BF16)).astype(BF16)
    for group in range(GROUPS):
        for srv in range(SRVS):
            at = PIECE * (SRVS * group + srv)
            for block in range(BLOCKS):
                slab_ref[group, srv, PIECE * block : PIECE * (block + 1), :] = f_ref[
                    block, at : at + PIECE, :
                ]
            dkv_ref[group, srv] = slab_ref[group, srv].astype(BF16)


def exchange(block, axis, groups=None):
    return lax.all_to_all(block, axis, 0, 0, tiled=True, axis_index_groups=groups)


def rotate(block, turn):
    pairs = [(q[i], q[(i + turn) % QUAD]) for q in NEAR for i in range(QUAD)]
    return lax.ppermute(block, "dp", pairs)


def local(queries, keys, values, output_gradient, doc_ids):
    rows = queries.shape[0] * queries.shape[1]
    part = GROUPS * PIECE
    wide = 2 * HEAD
    vmem = pl.BlockSpec(memory_space=pltpu.VMEM)
    smem = pl.BlockSpec(memory_space=pltpu.SMEM)
    params = pltpu.CompilerParams(vmem_limit_bytes=30 * 1024 * 1024)
    roomy = pltpu.CompilerParams(vmem_limit_bytes=60 * 1024 * 1024)
    call = functools.partial(pl.pallas_call, compiler_params=params)
    slabs_shape = (GROUPS, SRVS, BLOCKS * PIECE, wide)

    hbm = pl.BlockSpec(memory_space=pltpu.HBM)
    sources = (doc_ids.reshape(-1, 128), keys, values)
    packed = pl.pallas_call(
        pack_kernel,
        out_shape=jax.ShapeDtypeStruct((part + 8, wide), BF16),
        in_specs=[hbm] * 3,
        out_specs=vmem,
        scratch_shapes=[pltpu.VMEM(x.shape, x.dtype) for x in sources]
        + [
            pltpu.VMEM(keys.shape, F32),
            pltpu.VMEM(values.shape, F32),
            pltpu.VMEM((part + 8, wide), F32),
            pltpu.SemaphoreType.DMA((3,)),
        ],
        compiler_params=roomy,
        name="pack",
    )(*sources)
    gathered = lax.all_gather(packed, "dp", axis=0, axis_index_groups=FAR)
    slabs, qg = pl.pallas_call(
        fan_kernel,
        out_shape=(
            jax.ShapeDtypeStruct(slabs_shape, BF16),
            jax.ShapeDtypeStruct((rows + 8, wide), BF16),
        ),
        in_specs=[vmem, hbm, hbm],
        out_specs=(vmem, vmem),
        scratch_shapes=[
            pltpu.VMEM((QUAD, part + 8, wide), F32),
            pltpu.VMEM((GROUPS, BLOCKS * PIECE, wide), F32),
            pltpu.SemaphoreType.DMA((2,)),
        ],
        compiler_params=roomy,
        name="fan",
    )(gathered, queries.reshape(rows, HEAD), output_gradient.reshape(rows, HEAD))
    flat = (GROUPS * SRVS, BLOCKS * PIECE, wide)
    slabs = exchange(slabs.reshape(flat), ("head", "srv")).reshape(slabs_shape)
    qg = lax.all_gather(qg, "dp", axis=0, axis_index_groups=NEAR)

    e, o, stats, active, kv = call(
        forward_kernel,
        out_shape=(
            jax.ShapeDtypeStruct((BLOCKS, SHARD, QUAD * rows), BF16),
            jax.ShapeDtypeStruct((QUAD, HEAD, rows), F32),
            jax.ShapeDtypeStruct((QUAD, 4 * QUAD, rows), F32),
            jax.ShapeDtypeStruct((2,), jnp.int32),
            jax.ShapeDtypeStruct((BLOCKS, SHARD, wide), BF16),
        ),
        in_specs=[vmem] * 2,
        out_specs=(vmem, vmem, vmem, smem, vmem),
        scratch_shapes=[
            pltpu.VMEM((BLOCKS, SHARD, QUAD * rows), F32),
            pltpu.VMEM((QUAD, 8, rows), F32),
            pltpu.VMEM((QUAD, 8, rows), F32),
            pltpu.VMEM(slabs_shape, F32),
            pltpu.VMEM((BLOCKS, SHARD, wide), F32),
        ],
        name="forward",
    )(qg, slabs)
    stats = exchange(stats.reshape(QUAD * 4 * QUAD, rows), "dp", NEAR)
    stats = stats.reshape(QUAD, 4 * QUAD, rows)
    *oqs, dkv = call(
        backward_kernel,
        out_shape=(
            *[jax.ShapeDtypeStruct((rows, wide), BF16)] * QUAD,
            jax.ShapeDtypeStruct(slabs_shape, BF16),
        ),
        in_specs=[smem] + [vmem] * 5,
        out_specs=(vmem,) * 5,
        scratch_shapes=[
            pltpu.VMEM((QUAD, HEAD, rows), F32),
            pltpu.VMEM((BLOCKS, SHARD, wide), F32),
            pltpu.VMEM(slabs_shape, F32),
        ],
        name="backward",
    )(active, qg, kv, e, o, stats)

    oqs = [oqs[0]] + [rotate(oqs[turn], -turn) for turn in range(1, QUAD)]
    dkv = exchange(dkv.reshape(flat), ("head", "srv"))
    dkv, oqs = lax.optimization_barrier((dkv, oqs))
    dkv = call(
        fold_kernel,
        out_shape=jax.ShapeDtypeStruct((QUAD, part, wide), BF16),
        in_specs=[vmem],
        out_specs=vmem,
        scratch_shapes=[
            pltpu.VMEM((GROUPS, BLOCKS * PIECE, wide), F32),
            pltpu.VMEM((BLOCKS, part, wide), F32),
        ],
        name="fold",
    )(dkv.reshape(slabs_shape))
    dkv = exchange(dkv, "dp", FAR)
    k_grad, v_grad = call(
        finish_kernel,
        out_shape=(jax.ShapeDtypeStruct((PIECE, GROUPS * HEAD), BF16),) * 2,
        in_specs=[vmem],
        out_specs=(vmem, vmem),
        scratch_shapes=[pltpu.VMEM((part, wide), F32)],
        name="finish",
    )(dkv)

    oq = sum(x.astype(F32) for x in oqs).astype(BF16)
    attention = oq[:, :HEAD].reshape(queries.shape)
    q_grad = oq[:, HEAD:].reshape(queries.shape)
    return attention, q_grad, k_grad, v_grad


def solution(mesh):
    placed = (
        P("dp", "srv", "head"),
        P(("dp", "head"), None),
        P(("dp", "head"), None),
        P("dp", "srv", "head"),
        P("dp"),
    )
    return jax.shard_map(
        local,
        mesh=mesh,
        in_specs=placed,
        out_specs=(
            P("dp", "srv", "head"),
            P("dp", "srv", "head"),
            P(("dp", "head", "srv"), None),
            P(("dp", "head", "srv"), None),
        ),
        check_vma=False,
    )
```

```python
import functools

import jax
import jax.numpy as jnp
from jax import lax
from jax.experimental import pallas as pl
from jax.experimental.pallas import tpu as pltpu
from jax.sharding import PartitionSpec as P

HEAD = 128
DP = 16
QUAD = 4
BLOCKS = 3
SHARD = 640
CONTEXT = 8192
DOCS = 8
GROUPS = 8
SRVS = 4
PIECE = SHARD // GROUPS // SRVS
SCALE = HEAD**-0.5
EXP2_SCALE = SCALE * 1.4426950408889634
NEGATIVE = -1e30
NEAR = tuple(tuple(range(QUAD * q, QUAD * q + QUAD)) for q in range(DP // QUAD))
FAR = tuple(tuple(range(m, DP, QUAD)) for m in range(QUAD))

F32 = jnp.float32
BF16 = jnp.bfloat16
NT = (((1,), (1,)), ((), ()))
NN = (((1,), (0,)), ((), ()))


def dot(lhs, rhs, dims):
    return lax.dot_general(lhs, rhs, dims, preferred_element_type=F32)


def flip(block):
    size = block.shape[1]
    rows = lax.broadcasted_iota(jnp.int32, (size, size), 0)
    columns = lax.broadcasted_iota(jnp.int32, (size, size), 1)
    return dot((rows == columns).astype(BF16), block, NT)


def fold8(block, op):
    rows, cols = block.shape
    return op(block.reshape(rows // 8, 8, cols), axis=0)


def member_of(member, turn):
    return lax.rem(member - turn + QUAD, QUAD)


def fetch(sources, targets, sems):
    copies = [
        pltpu.make_async_copy(source, target, sems.at[i])
        for i, (source, target) in enumerate(zip(sources, targets))
    ]
    for copy in copies:
        copy.start()
    return copies


def pack_kernel(
    docs_in, keys_in, values_in, out_ref, docs, keys, values, k_ref, v_ref, f_ref, sems
):
    srv = lax.axis_index("srv")
    for copy in fetch((docs_in, keys_in, values_in), (docs, keys, values), sems):
        copy.wait()
    k_ref[...] = keys[...].astype(F32)
    v_ref[...] = values[...].astype(F32)

    def mine(ref):
        piece = ref[:PIECE, :]
        for part in range(1, SRVS):
            other = ref[PIECE * part : PIECE * (part + 1), :]
            piece = jnp.where(srv == part, other, piece)
        return piece

    k, v = mine(k_ref), mine(v_ref)
    for group in range(GROUPS):
        span = slice(PIECE * group, PIECE * (group + 1))
        columns = slice(HEAD * group, HEAD * (group + 1))
        f_ref[span, :HEAD] = k[:, columns]
        f_ref[span, HEAD:] = v[:, columns]
    lanes = lax.broadcasted_iota(jnp.int32, (8, 2 * HEAD), 1)
    row = jnp.zeros((8, 2 * HEAD), F32)
    for doc in range(DOCS):
        count = jnp.sum(jnp.where(docs[...] == doc, 1.0, 0.0), axis=1, keepdims=True)
        count = jnp.sum(count, axis=0, keepdims=True).astype(jnp.int32)
        row = jnp.where(lanes == doc, (count >> 6).astype(F32), row)
        row = jnp.where(lanes == DOCS + doc, (count & 63).astype(F32), row)
    first = lax.broadcasted_iota(jnp.int32, (8, 2 * HEAD), 0) == 0
    f_ref[PIECE * GROUPS :, :] = jnp.where(first, row, 0.0)
    out_ref[...] = f_ref[...].astype(BF16)


def fan_kernel(gathered, queries, gradient, out_ref, qg_ref, f_ref, slab_ref, sems):
    rows = queries.shape[0]
    targets = (qg_ref.at[pl.ds(0, rows), pl.ds(0, HEAD)], qg_ref.at[pl.ds(0, rows), pl.ds(HEAD, HEAD)])
    copies = fetch((queries, gradient), targets, sems)
    for quad in range(QUAD):
        f_ref[quad] = gathered[quad].astype(F32)
    for group in range(GROUPS):
        for block in range(BLOCKS):
            slab_ref[group, PIECE * block : PIECE * (block + 1), :] = f_ref[
                block + 1, PIECE * group : PIECE * (group + 1), :
            ]
        slab = slab_ref[group].astype(BF16)
        for srv in range(SRVS):
            out_ref[group, srv] = slab
    count = sum(f_ref[quad, PIECE * GROUPS :, :] for quad in range(QUAD))
    qg_ref[rows:, :] = count.astype(BF16)
    for copy in copies:
        copy.wait()


def fold_kernel(parts, own_ref, next_ref, far_ref, last_ref, slab_ref, f_ref):
    quad = lax.axis_index("dp") // QUAD
    for group in range(GROUPS):
        slab_ref[group] = sum(parts[group, srv].astype(F32) for srv in range(SRVS))
        for block in range(BLOCKS):
            f_ref[block, PIECE * group : PIECE * (group + 1), :] = slab_ref[
                group, PIECE * block : PIECE * (block + 1), :
            ]
    for turn, ref in enumerate((own_ref, next_ref, far_ref, last_ref)):
        owner = lax.rem(quad + turn, QUAD)
        ref[...] = f_ref[jnp.maximum(owner - 1, 0)].astype(BF16)

    @pl.when(quad == 0)
    def _():
        own_ref[...] = jnp.zeros(own_ref.shape, BF16)


def finish_kernel(p0, p1, p2, p3, k_ref, v_ref, f_ref):
    f_ref[...] = sum(part[...].astype(F32) for part in (p0, p1, p2, p3))
    for group in range(GROUPS):
        span = slice(PIECE * group, PIECE * (group + 1))
        columns = slice(HEAD * group, HEAD * (group + 1))
        k_ref[:, columns] = f_ref[span, :HEAD].astype(BF16)
        v_ref[:, columns] = f_ref[span, HEAD:].astype(BF16)


def forward_kernel(
    qg, slabs, e_ref, o_ref, stats_ref, active, kv, s_ref, m_ref, l_ref, slab_ref, f_ref
):
    dp = lax.axis_index("dp")
    quad, member = dp // QUAD, dp % QUAD
    qs = [qg.at[member_of(member, turn)] for turn in range(QUAD)]
    cols = o_ref.shape[2]
    keys = kv.shape[1]
    query_at = CONTEXT + 2 * cols * quad

    count = sum(jnp.sum(qg[who, cols:, :].astype(F32), axis=0, keepdims=True) for who in range(QUAD))
    lanes = lax.broadcasted_iota(jnp.int32, count.shape, 1)
    starts = []
    for doc in range(DOCS):
        high = jnp.sum(jnp.where(lanes < doc, count, 0.0)) * 64.0
        low = jnp.sum(jnp.where((lanes >= DOCS) & (lanes < DOCS + doc), count, 0.0))
        starts.append((high + low).astype(jnp.int32))
    reach = jnp.int32(0)
    for start in starts:
        reach = jnp.where(start <= query_at, jnp.maximum(reach, start), reach)
    first, last = jnp.int32(0), jnp.int32(0)
    for block in range(BLOCKS):
        shard = SHARD * (QUAD * (block + 1) + member)
        first += (shard + SHARD <= reach).astype(jnp.int32)
        last += (shard < query_at + 2 * cols).astype(jnp.int32)
    active[0] = first
    active[1] = last

    for group in range(GROUPS):
        for srv in range(SRVS):
            slab_ref[group, srv] = slabs[group, srv].astype(F32)
            at = PIECE * (SRVS * group + srv)
            for block in range(BLOCKS):
                f_ref[block, at : at + PIECE, :] = slab_ref[
                    group, srv, PIECE * block : PIECE * (block + 1), :
                ]
    for block in range(BLOCKS):
        kv[block] = f_ref[block].astype(BF16)

    pattern = lax.broadcasted_iota(jnp.int32, (keys, cols), 0) + SHARD * (QUAD + member)
    lane = lax.broadcasted_iota(jnp.int32, (1, cols), 1)
    m_ref[...] = jnp.full(m_ref.shape, NEGATIVE, F32)
    l_ref[...] = jnp.zeros(l_ref.shape, F32)
    o_ref[...] = jnp.zeros(o_ref.shape, F32)
    query_places, doc_starts = [], []
    for turn in range(QUAD):
        query_place = query_at + (cols // 2) * member_of(member, turn) + lane // 2
        doc_start = jnp.zeros_like(query_place)
        for start in starts:
            doc_start = jnp.where(start <= query_place, jnp.maximum(doc_start, start), doc_start)
        query_places.append(query_place)
        doc_starts.append(doc_start)

    def scores(t, carry):
        k = kv[t, :, :HEAD]
        key_place = pattern + QUAD * SHARD * t
        for turn in range(QUAD):
            span = pl.ds(turn * cols, cols)
            s = dot(k, qs[turn][:cols, :HEAD], NT)
            allowed = (key_place >= doc_starts[turn]) & (key_place <= query_places[turn])
            s = jnp.where(allowed, s, NEGATIVE)
            s_ref[t, :, span] = s
            m_ref[turn] = jnp.maximum(m_ref[turn], fold8(s, jnp.max))
        return carry

    lax.fori_loop(first, last, scores, 0)
    tops = [jnp.max(m_ref[turn], axis=0, keepdims=True) for turn in range(QUAD)]

    def weigh(t, carry):
        v = flip(kv[t, :, HEAD:]).astype(BF16)
        for turn in range(QUAD):
            span = pl.ds(turn * cols, cols)
            e = jnp.exp2((s_ref[t, :, span] - tops[turn]) * EXP2_SCALE)
            l_ref[turn] += fold8(e, jnp.sum)
            e = e.astype(BF16)
            e_ref[t, :, span] = e
            o_ref[turn] += dot(v, e, NN)
        return carry

    lax.fori_loop(first, last, weigh, 0)
    for turn in range(QUAD):
        tile = member_of(member, turn)
        gradient = flip(qs[turn][:cols, HEAD:])
        norm = jnp.sum(l_ref[turn], axis=0, keepdims=True)
        delta = jnp.sum(gradient * o_ref[turn], axis=0, keepdims=True)
        for copy in range(QUAD):
            stats_ref[copy, pl.ds(tile, 1), :] = tops[turn]
            stats_ref[copy, pl.ds(QUAD + tile, 1), :] = norm
            stats_ref[copy, pl.ds(2 * QUAD + tile, 1), :] = delta
            stats_ref[copy, pl.ds(3 * QUAD + tile, 1), :] = jnp.zeros_like(norm)


def backward_kernel(
    active, qg, kv, e_ref, o_ref, stats, oq0, oq1, oq2, oq3, dkv_ref, dq_ref, f_ref, slab_ref
):
    member = lax.axis_index("dp") % QUAD
    first, last = active[0], active[1]
    qs = [qg.at[member_of(member, turn)] for turn in range(QUAD)]
    oqs = (oq0, oq1, oq2, oq3)
    cols = o_ref.shape[2]
    keys = kv.shape[1]
    dq_ref[...] = jnp.zeros(dq_ref.shape, F32)
    shares, deltas = [], []
    for turn in range(QUAD):
        tile = member_of(member, turn)
        row = lambda who, kind: stats[who, pl.ds(kind * QUAD + tile, 1), :]
        top = functools.reduce(jnp.maximum, [row(who, 0) for who in range(QUAD)])
        weights = [jnp.exp2((row(who, 0) - top) * EXP2_SCALE) for who in range(QUAD)]
        norm = sum(weights[who] * row(who, 1) for who in range(QUAD))
        deltas.append(sum(weights[who] * row(who, 2) for who in range(QUAD)) / norm)
        shares.append(jnp.exp2((row(member, 0) - top) * EXP2_SCALE) / norm)

    def clear(t, carry):
        f_ref[t] = jnp.zeros((keys, 2 * HEAD), F32)
        return carry

    lax.fori_loop(0, first, clear, 0)
    lax.fori_loop(last, BLOCKS, clear, 0)

    def grads(t, carry):
        k = kv[t, :, :HEAD]
        v = kv[t, :, HEAD:]
        kt = flip(k).astype(BF16)
        dk = jnp.zeros((keys, HEAD), F32)
        dv = jnp.zeros((keys, HEAD), F32)
        for turn in range(QUAD):
            q, gradient = qs[turn][:cols, :HEAD], qs[turn][:cols, HEAD:]
            p = e_ref[t, :, pl.ds(turn * cols, cols)].astype(F32) * shares[turn]
            ds = (p * (dot(v, gradient, NT) - deltas[turn])).astype(BF16)
            dv += dot(p.astype(BF16), gradient, NN)
            dk += dot(ds, q, NN)
            dq_ref[turn] += dot(kt, ds, NN)
        f_ref[t, :, :HEAD] = dk * SCALE
        f_ref[t, :, HEAD:] = dv
        return carry

    lax.fori_loop(first, last, grads, 0)
    for turn in range(QUAD):
        oqs[turn][:, :HEAD] = flip((o_ref[turn] * shares[turn]).astype(BF16)).astype(BF16)
        oqs[turn][:, HEAD:] = flip((dq_ref[turn] * SCALE).astype(BF16)).astype(BF16)
    for group in range(GROUPS):
        for srv in range(SRVS):
            at = PIECE * (SRVS * group + srv)
            for block in range(BLOCKS):
                slab_ref[group, srv, PIECE * block : PIECE * (block + 1), :] = f_ref[
                    block, at : at + PIECE, :
                ]
            dkv_ref[group, srv] = slab_ref[group, srv].astype(BF16)


def exchange(block, axis, groups=None):
    return lax.all_to_all(block, axis, 0, 0, tiled=True, axis_index_groups=groups)


def rotate(block, turn):
    pairs = [(q[i], q[(i + turn) % QUAD]) for q in NEAR for i in range(QUAD)]
    return lax.ppermute(block, "dp", pairs)


def carry_on(block, turn):
    pairs = [
        (QUAD * quad + m, QUAD * ((quad + turn) % QUAD) + m)
        for quad in range(QUAD)
        for m in range(QUAD)
        if (quad + turn) % QUAD
    ]
    return lax.ppermute(block, "dp", pairs)


def local(queries, keys, values, output_gradient, doc_ids):
    rows = queries.shape[0] * queries.shape[1]
    part = GROUPS * PIECE
    wide = 2 * HEAD
    vmem = pl.BlockSpec(memory_space=pltpu.VMEM)
    smem = pl.BlockSpec(memory_space=pltpu.SMEM)
    params = pltpu.CompilerParams(vmem_limit_bytes=30 * 1024 * 1024)
    roomy = pltpu.CompilerParams(vmem_limit_bytes=60 * 1024 * 1024)
    call = functools.partial(pl.pallas_call, compiler_params=params)
    slabs_shape = (GROUPS, SRVS, BLOCKS * PIECE, wide)

    hbm = pl.BlockSpec(memory_space=pltpu.HBM)
    sources = (doc_ids.reshape(-1, 128), keys, values)
    packed = pl.pallas_call(
        pack_kernel,
        out_shape=jax.ShapeDtypeStruct((part + 8, wide), BF16),
        in_specs=[hbm] * 3,
        out_specs=vmem,
        scratch_shapes=[pltpu.VMEM(x.shape, x.dtype) for x in sources]
        + [
            pltpu.VMEM(keys.shape, F32),
            pltpu.VMEM(values.shape, F32),
            pltpu.VMEM((part + 8, wide), F32),
            pltpu.SemaphoreType.DMA((3,)),
        ],
        compiler_params=roomy,
        name="pack",
    )(*sources)
    gathered = lax.all_gather(packed, "dp", axis=0, axis_index_groups=FAR)
    slabs, qg = pl.pallas_call(
        fan_kernel,
        out_shape=(
            jax.ShapeDtypeStruct(slabs_shape, BF16),
            jax.ShapeDtypeStruct((rows + 8, wide), BF16),
        ),
        in_specs=[vmem, hbm, hbm],
        out_specs=(vmem, vmem),
        scratch_shapes=[
            pltpu.VMEM((QUAD, part + 8, wide), F32),
            pltpu.VMEM((GROUPS, BLOCKS * PIECE, wide), F32),
            pltpu.SemaphoreType.DMA((2,)),
        ],
        compiler_params=roomy,
        name="fan",
    )(gathered, queries.reshape(rows, HEAD), output_gradient.reshape(rows, HEAD))
    flat = (GROUPS * SRVS, BLOCKS * PIECE, wide)
    slabs = exchange(slabs.reshape(flat), ("head", "srv")).reshape(slabs_shape)
    qg = lax.all_gather(qg, "dp", axis=0, axis_index_groups=NEAR)

    e, o, stats, active, kv = call(
        forward_kernel,
        out_shape=(
            jax.ShapeDtypeStruct((BLOCKS, SHARD, QUAD * rows), BF16),
            jax.ShapeDtypeStruct((QUAD, HEAD, rows), F32),
            jax.ShapeDtypeStruct((QUAD, 4 * QUAD, rows), F32),
            jax.ShapeDtypeStruct((2,), jnp.int32),
            jax.ShapeDtypeStruct((BLOCKS, SHARD, wide), BF16),
        ),
        in_specs=[vmem] * 2,
        out_specs=(vmem, vmem, vmem, smem, vmem),
        scratch_shapes=[
            pltpu.VMEM((BLOCKS, SHARD, QUAD * rows), F32),
            pltpu.VMEM((QUAD, 8, rows), F32),
            pltpu.VMEM((QUAD, 8, rows), F32),
            pltpu.VMEM(slabs_shape, F32),
            pltpu.VMEM((BLOCKS, SHARD, wide), F32),
        ],
        name="forward",
    )(qg, slabs)
    stats = exchange(stats.reshape(QUAD * 4 * QUAD, rows), "dp", NEAR)
    stats = stats.reshape(QUAD, 4 * QUAD, rows)
    *oqs, dkv = call(
        backward_kernel,
        out_shape=(
            *[jax.ShapeDtypeStruct((rows, wide), BF16)] * QUAD,
            jax.ShapeDtypeStruct(slabs_shape, BF16),
        ),
        in_specs=[smem] + [vmem] * 5,
        out_specs=(vmem,) * 5,
        scratch_shapes=[
            pltpu.VMEM((QUAD, HEAD, rows), F32),
            pltpu.VMEM((BLOCKS, SHARD, wide), F32),
            pltpu.VMEM(slabs_shape, F32),
        ],
        name="backward",
    )(active, qg, kv, e, o, stats)

    oqs = [oqs[0]] + [rotate(oqs[turn], -turn) for turn in range(1, QUAD)]
    dkv = exchange(dkv.reshape(flat), ("head", "srv"))
    dkv, oqs = lax.optimization_barrier((dkv, oqs))
    dkv = call(
        fold_kernel,
        out_shape=(jax.ShapeDtypeStruct((part, wide), BF16),) * QUAD,
        in_specs=[vmem],
        out_specs=(vmem,) * QUAD,
        scratch_shapes=[
            pltpu.VMEM((GROUPS, BLOCKS * PIECE, wide), F32),
            pltpu.VMEM((BLOCKS, part, wide), F32),
        ],
        name="fold",
    )(dkv.reshape(slabs_shape))
    dkv = [dkv[0]] + [carry_on(dkv[turn], turn) for turn in range(1, QUAD)]
    k_grad, v_grad = call(
        finish_kernel,
        out_shape=(jax.ShapeDtypeStruct((PIECE, GROUPS * HEAD), BF16),) * 2,
        in_specs=[vmem] * QUAD,
        out_specs=(vmem, vmem),
        scratch_shapes=[pltpu.VMEM((part, wide), F32)],
        name="finish",
    )(*dkv)

    oq = sum(x.astype(F32) for x in oqs).astype(BF16)
    attention = oq[:, :HEAD].reshape(queries.shape)
    q_grad = oq[:, HEAD:].reshape(queries.shape)
    return attention, q_grad, k_grad, v_grad


def solution(mesh):
    placed = (
        P("dp", "srv", "head"),
        P(("dp", "head"), None),
        P(("dp", "head"), None),
        P("dp", "srv", "head"),
        P("dp"),
    )
    return jax.shard_map(
        local,
        mesh=mesh,
        in_specs=placed,
        out_specs=(
            P("dp", "srv", "head"),
            P("dp", "srv", "head"),
            P(("dp", "head", "srv"), None),
            P(("dp", "head", "srv"), None),
        ),
        check_vma=False,
    )
```

```python
import functools

import jax
import jax.numpy as jnp
from jax import lax
from jax.experimental import pallas as pl
from jax.experimental.pallas import tpu as pltpu
from jax.sharding import PartitionSpec as P

HEAD = 128
DP = 16
QUAD = 4
BLOCKS = 3
SHARD = 640
CONTEXT = 8192
ROWS = 512
DOC_MAX = 5120
DOCS = 8
GROUPS = 8
SRVS = 4
PIECE = SHARD // GROUPS // SRVS
SCALE = HEAD**-0.5
EXP2_SCALE = SCALE * 1.4426950408889634
NEGATIVE = -1e30
NEAR = tuple(tuple(range(QUAD * q, QUAD * q + QUAD)) for q in range(DP // QUAD))
FAR = tuple(tuple(range(m, DP, QUAD)) for m in range(QUAD))

F32 = jnp.float32
BF16 = jnp.bfloat16
NT = (((1,), (1,)), ((), ()))
NN = (((1,), (0,)), ((), ()))


def dot(lhs, rhs, dims):
    return lax.dot_general(lhs, rhs, dims, preferred_element_type=F32)


def flip(block):
    size = block.shape[1]
    rows = lax.broadcasted_iota(jnp.int32, (size, size), 0)
    columns = lax.broadcasted_iota(jnp.int32, (size, size), 1)
    return dot((rows == columns).astype(BF16), block, NT)


def fold8(block, op):
    rows, cols = block.shape
    return op(block.reshape(rows // 8, 8, cols), axis=0)


def member_of(member, turn):
    return lax.rem(member - turn + QUAD, QUAD)


def fetch(sources, targets, sems):
    copies = [
        pltpu.make_async_copy(source, target, sems.at[i])
        for i, (source, target) in enumerate(zip(sources, targets))
    ]
    for copy in copies:
        copy.start()
    return copies


def pack_kernel(
    docs_in, keys_in, values_in, out_ref, docs, keys, values, k_ref, v_ref, f_ref, sems
):
    srv = lax.axis_index("srv")
    for copy in fetch((docs_in, keys_in, values_in), (docs, keys, values), sems):
        copy.wait()
    k_ref[...] = keys[...].astype(F32)
    v_ref[...] = values[...].astype(F32)

    def mine(ref):
        piece = ref[:PIECE, :]
        for part in range(1, SRVS):
            other = ref[PIECE * part : PIECE * (part + 1), :]
            piece = jnp.where(srv == part, other, piece)
        return piece

    k, v = mine(k_ref), mine(v_ref)
    for group in range(GROUPS):
        span = slice(PIECE * group, PIECE * (group + 1))
        columns = slice(HEAD * group, HEAD * (group + 1))
        f_ref[span, :HEAD] = k[:, columns]
        f_ref[span, HEAD:] = v[:, columns]
    lanes = lax.broadcasted_iota(jnp.int32, (8, 2 * HEAD), 1)
    row = jnp.zeros((8, 2 * HEAD), F32)
    for doc in range(DOCS):
        count = jnp.sum(jnp.where(docs[...] == doc, 1.0, 0.0), axis=1, keepdims=True)
        count = jnp.sum(count, axis=0, keepdims=True).astype(jnp.int32)
        row = jnp.where(lanes == doc, (count >> 6).astype(F32), row)
        row = jnp.where(lanes == DOCS + doc, (count & 63).astype(F32), row)
    first = lax.broadcasted_iota(jnp.int32, (8, 2 * HEAD), 0) == 0
    f_ref[PIECE * GROUPS :, :] = jnp.where(first, row, 0.0)
    out_ref[...] = f_ref[...].astype(BF16)


def fan_kernel(gathered, queries, gradient, out_ref, qg_ref, f_ref, slab_ref, sems):
    rows = queries.shape[0]
    targets = (qg_ref.at[pl.ds(0, rows), pl.ds(0, HEAD)], qg_ref.at[pl.ds(0, rows), pl.ds(HEAD, HEAD)])
    copies = fetch((queries, gradient), targets, sems)
    for quad in range(QUAD):
        f_ref[quad] = gathered[quad].astype(F32)
    for group in range(GROUPS):
        for block in range(BLOCKS):
            slab_ref[group, PIECE * block : PIECE * (block + 1), :] = f_ref[
                block + 1, PIECE * group : PIECE * (group + 1), :
            ]
        slab = slab_ref[group].astype(BF16)
        for srv in range(SRVS):
            out_ref[group, srv] = slab
    count = sum(f_ref[quad, PIECE * GROUPS :, :] for quad in range(QUAD))
    qg_ref[rows:, :] = count.astype(BF16)
    for copy in copies:
        copy.wait()


def fold_kernel(parts, own_ref, next_ref, far_ref, last_ref, slab_ref, f_ref):
    quad = lax.axis_index("dp") // QUAD
    for group in range(GROUPS):
        slab_ref[group] = sum(parts[group, srv].astype(F32) for srv in range(SRVS))
        for block in range(BLOCKS):
            f_ref[block, PIECE * group : PIECE * (group + 1), :] = slab_ref[
                group, PIECE * block : PIECE * (block + 1), :
            ]
    for turn, ref in enumerate((own_ref, next_ref, far_ref, last_ref)):
        owner = lax.rem(quad + turn, QUAD)
        ref[...] = f_ref[jnp.maximum(owner - 1, 0)].astype(BF16)

    @pl.when(quad == 0)
    def _():
        own_ref[...] = jnp.zeros(own_ref.shape, BF16)


def finish_kernel(p0, p1, p2, p3, k_ref, v_ref, f_ref):
    f_ref[...] = sum(part[...].astype(F32) for part in (p0, p1, p2, p3))
    for group in range(GROUPS):
        span = slice(PIECE * group, PIECE * (group + 1))
        columns = slice(HEAD * group, HEAD * (group + 1))
        k_ref[:, columns] = f_ref[span, :HEAD].astype(BF16)
        v_ref[:, columns] = f_ref[span, HEAD:].astype(BF16)


def forward_kernel(
    qg, slabs, e_ref, o_ref, stats_ref, active, kv, s_ref, m_ref, l_ref, slab_ref, f_ref
):
    dp = lax.axis_index("dp")
    quad, member = dp // QUAD, dp % QUAD
    qs = [qg.at[member_of(member, turn)] for turn in range(QUAD)]
    cols = o_ref.shape[2]
    keys = kv.shape[1]
    query_at = CONTEXT + 2 * cols * quad

    count = sum(jnp.sum(qg[who, cols:, :].astype(F32), axis=0, keepdims=True) for who in range(QUAD))
    lanes = lax.broadcasted_iota(jnp.int32, count.shape, 1)
    starts = []
    for doc in range(DOCS):
        high = jnp.sum(jnp.where(lanes < doc, count, 0.0)) * 64.0
        low = jnp.sum(jnp.where((lanes >= DOCS) & (lanes < DOCS + doc), count, 0.0))
        starts.append((high + low).astype(jnp.int32))
    reach = jnp.int32(0)
    for start in starts:
        reach = jnp.where(start <= query_at, jnp.maximum(reach, start), reach)
    first, last = jnp.int32(0), jnp.int32(0)
    for block in range(BLOCKS):
        shard = SHARD * (QUAD * (block + 1) + member)
        first += (shard + SHARD <= reach).astype(jnp.int32)
        last += (shard < query_at + 2 * cols).astype(jnp.int32)
    active[0] = first
    active[1] = last

    for group in range(GROUPS):
        for srv in range(SRVS):
            slab_ref[group, srv] = slabs[group, srv].astype(F32)
            at = PIECE * (SRVS * group + srv)
            for block in range(BLOCKS):
                f_ref[block, at : at + PIECE, :] = slab_ref[
                    group, srv, PIECE * block : PIECE * (block + 1), :
                ]
    for block in range(BLOCKS):
        kv[block] = f_ref[block].astype(BF16)

    pattern = lax.broadcasted_iota(jnp.int32, (keys, cols), 0) + SHARD * (QUAD + member)
    lane = lax.broadcasted_iota(jnp.int32, (1, cols), 1)
    m_ref[...] = jnp.full(m_ref.shape, NEGATIVE, F32)
    l_ref[...] = jnp.zeros(l_ref.shape, F32)
    o_ref[...] = jnp.zeros(o_ref.shape, F32)
    query_places, doc_starts = [], []
    for turn in range(QUAD):
        query_place = query_at + (cols // 2) * member_of(member, turn) + lane // 2
        doc_start = jnp.zeros_like(query_place)
        for start in starts:
            doc_start = jnp.where(start <= query_place, jnp.maximum(doc_start, start), doc_start)
        query_places.append(query_place)
        doc_starts.append(doc_start)

    def scores(t, carry):
        k = kv[t, :, :HEAD]
        key_place = pattern + QUAD * SHARD * t
        for turn in range(QUAD):
            span = pl.ds(turn * cols, cols)
            s = dot(k, qs[turn][:cols, :HEAD], NT)
            allowed = (key_place >= doc_starts[turn]) & (key_place <= query_places[turn])
            s = jnp.where(allowed, s, NEGATIVE)
            s_ref[t, :, span] = s
            m_ref[turn] = jnp.maximum(m_ref[turn], fold8(s, jnp.max))
        return carry

    lax.fori_loop(first, last, scores, 0)
    tops = [jnp.max(m_ref[turn], axis=0, keepdims=True) for turn in range(QUAD)]

    def weigh(t, carry):
        v = flip(kv[t, :, HEAD:]).astype(BF16)
        for turn in range(QUAD):
            span = pl.ds(turn * cols, cols)
            e = jnp.exp2((s_ref[t, :, span] - tops[turn]) * EXP2_SCALE)
            l_ref[turn] += fold8(e, jnp.sum)
            e = e.astype(BF16)
            e_ref[t, :, span] = e
            o_ref[turn] += dot(v, e, NN)
        return carry

    lax.fori_loop(first, last, weigh, 0)
    for turn in range(QUAD):
        tile = member_of(member, turn)
        gradient = flip(qs[turn][:cols, HEAD:])
        norm = jnp.sum(l_ref[turn], axis=0, keepdims=True)
        delta = jnp.sum(gradient * o_ref[turn], axis=0, keepdims=True)
        for copy in range(QUAD):
            stats_ref[copy, pl.ds(tile, 1), :] = tops[turn]
            stats_ref[copy, pl.ds(QUAD + tile, 1), :] = norm
            stats_ref[copy, pl.ds(2 * QUAD + tile, 1), :] = delta
            stats_ref[copy, pl.ds(3 * QUAD + tile, 1), :] = jnp.zeros_like(norm)


def backward_kernel(
    active, qg, kv, e_ref, o_ref, stats, oq0, oq1, oq2, oq3, dkv_ref, dq_ref, f_ref, slab_ref
):
    member = lax.axis_index("dp") % QUAD
    first, last = active[0], active[1]
    qs = [qg.at[member_of(member, turn)] for turn in range(QUAD)]
    oqs = (oq0, oq1, oq2, oq3)
    cols = o_ref.shape[2]
    keys = kv.shape[1]
    dq_ref[...] = jnp.zeros(dq_ref.shape, F32)
    shares, deltas = [], []
    for turn in range(QUAD):
        tile = member_of(member, turn)
        row = lambda who, kind: stats[who, pl.ds(kind * QUAD + tile, 1), :]
        top = functools.reduce(jnp.maximum, [row(who, 0) for who in range(QUAD)])
        weights = [jnp.exp2((row(who, 0) - top) * EXP2_SCALE) for who in range(QUAD)]
        norm = sum(weights[who] * row(who, 1) for who in range(QUAD))
        deltas.append(sum(weights[who] * row(who, 2) for who in range(QUAD)) / norm)
        shares.append(jnp.exp2((row(member, 0) - top) * EXP2_SCALE) / norm)

    def clear(t, carry):
        f_ref[t] = jnp.zeros((keys, 2 * HEAD), F32)
        return carry

    lax.fori_loop(0, first, clear, 0)
    lax.fori_loop(last, BLOCKS, clear, 0)

    def grads(t, carry):
        k = kv[t, :, :HEAD]
        v = kv[t, :, HEAD:]
        kt = flip(k).astype(BF16)
        dk = jnp.zeros((keys, HEAD), F32)
        dv = jnp.zeros((keys, HEAD), F32)
        for turn in range(QUAD):
            q, gradient = qs[turn][:cols, :HEAD], qs[turn][:cols, HEAD:]
            p = e_ref[t, :, pl.ds(turn * cols, cols)].astype(F32) * shares[turn]
            ds = (p * (dot(v, gradient, NT) - deltas[turn])).astype(BF16)
            dv += dot(p.astype(BF16), gradient, NN)
            dk += dot(ds, q, NN)
            dq_ref[turn] += dot(kt, ds, NN)
        f_ref[t, :, :HEAD] = dk * SCALE
        f_ref[t, :, HEAD:] = dv
        return carry

    lax.fori_loop(first, last, grads, 0)
    for turn in range(QUAD):
        oqs[turn][:, :HEAD] = flip((o_ref[turn] * shares[turn]).astype(BF16)).astype(BF16)
        oqs[turn][:, HEAD:] = flip((dq_ref[turn] * SCALE).astype(BF16)).astype(BF16)
    for group in range(GROUPS):
        for srv in range(SRVS):
            at = PIECE * (SRVS * group + srv)
            for block in range(BLOCKS):
                slab_ref[group, srv, PIECE * block : PIECE * (block + 1), :] = f_ref[
                    block, at : at + PIECE, :
                ]
            dkv_ref[group, srv] = slab_ref[group, srv].astype(BF16)


def exchange(block, axis, groups=None):
    return lax.all_to_all(block, axis, 0, 0, tiled=True, axis_index_groups=groups)


def rotate(block, turn):
    pairs = [(q[i], q[(i + turn) % QUAD]) for q in NEAR for i in range(QUAD)]
    return lax.ppermute(block, "dp", pairs)


def reached(quad, shard):
    first = CONTEXT + ROWS * quad
    return first - (DOC_MAX - 1) < SHARD * (shard + 1) and SHARD * shard < first + ROWS


def carry_on(block, turn):
    pairs = []
    for quad in range(QUAD):
        owner = (quad + turn) % QUAD
        for m in range(QUAD):
            if reached(quad, QUAD * owner + m):
                pairs.append((QUAD * quad + m, QUAD * owner + m))
    return lax.ppermute(block, "dp", pairs)


def local(queries, keys, values, output_gradient, doc_ids):
    rows = queries.shape[0] * queries.shape[1]
    part = GROUPS * PIECE
    wide = 2 * HEAD
    vmem = pl.BlockSpec(memory_space=pltpu.VMEM)
    smem = pl.BlockSpec(memory_space=pltpu.SMEM)
    params = pltpu.CompilerParams(vmem_limit_bytes=30 * 1024 * 1024)
    roomy = pltpu.CompilerParams(vmem_limit_bytes=60 * 1024 * 1024)
    call = functools.partial(pl.pallas_call, compiler_params=params)
    slabs_shape = (GROUPS, SRVS, BLOCKS * PIECE, wide)

    hbm = pl.BlockSpec(memory_space=pltpu.HBM)
    sources = (doc_ids.reshape(-1, 128), keys, values)
    packed = pl.pallas_call(
        pack_kernel,
        out_shape=jax.ShapeDtypeStruct((part + 8, wide), BF16),
        in_specs=[hbm] * 3,
        out_specs=vmem,
        scratch_shapes=[pltpu.VMEM(x.shape, x.dtype) for x in sources]
        + [
            pltpu.VMEM(keys.shape, F32),
            pltpu.VMEM(values.shape, F32),
            pltpu.VMEM((part + 8, wide), F32),
            pltpu.SemaphoreType.DMA((3,)),
        ],
        compiler_params=roomy,
        name="pack",
    )(*sources)
    gathered = lax.all_gather(packed, "dp", axis=0, axis_index_groups=FAR)
    slabs, qg = pl.pallas_call(
        fan_kernel,
        out_shape=(
            jax.ShapeDtypeStruct(slabs_shape, BF16),
            jax.ShapeDtypeStruct((rows + 8, wide), BF16),
        ),
        in_specs=[vmem, hbm, hbm],
        out_specs=(vmem, vmem),
        scratch_shapes=[
            pltpu.VMEM((QUAD, part + 8, wide), F32),
            pltpu.VMEM((GROUPS, BLOCKS * PIECE, wide), F32),
            pltpu.SemaphoreType.DMA((2,)),
        ],
        compiler_params=roomy,
        name="fan",
    )(gathered, queries.reshape(rows, HEAD), output_gradient.reshape(rows, HEAD))
    flat = (GROUPS * SRVS, BLOCKS * PIECE, wide)
    slabs = exchange(slabs.reshape(flat), ("head", "srv")).reshape(slabs_shape)
    qg = lax.all_gather(qg, "dp", axis=0, axis_index_groups=NEAR)

    e, o, stats, active, kv = call(
        forward_kernel,
        out_shape=(
            jax.ShapeDtypeStruct((BLOCKS, SHARD, QUAD * rows), BF16),
            jax.ShapeDtypeStruct((QUAD, HEAD, rows), F32),
            jax.ShapeDtypeStruct((QUAD, 4 * QUAD, rows), F32),
            jax.ShapeDtypeStruct((2,), jnp.int32),
            jax.ShapeDtypeStruct((BLOCKS, SHARD, wide), BF16),
        ),
        in_specs=[vmem] * 2,
        out_specs=(vmem, vmem, vmem, smem, vmem),
        scratch_shapes=[
            pltpu.VMEM((BLOCKS, SHARD, QUAD * rows), F32),
            pltpu.VMEM((QUAD, 8, rows), F32),
            pltpu.VMEM((QUAD, 8, rows), F32),
            pltpu.VMEM(slabs_shape, F32),
            pltpu.VMEM((BLOCKS, SHARD, wide), F32),
        ],
        name="forward",
    )(qg, slabs)
    stats = exchange(stats.reshape(QUAD * 4 * QUAD, rows), "dp", NEAR)
    stats = stats.reshape(QUAD, 4 * QUAD, rows)
    *oqs, dkv = call(
        backward_kernel,
        out_shape=(
            *[jax.ShapeDtypeStruct((rows, wide), BF16)] * QUAD,
            jax.ShapeDtypeStruct(slabs_shape, BF16),
        ),
        in_specs=[smem] + [vmem] * 5,
        out_specs=(vmem,) * 5,
        scratch_shapes=[
            pltpu.VMEM((QUAD, HEAD, rows), F32),
            pltpu.VMEM((BLOCKS, SHARD, wide), F32),
            pltpu.VMEM(slabs_shape, F32),
        ],
        name="backward",
    )(active, qg, kv, e, o, stats)

    oqs = [oqs[0]] + [rotate(oqs[turn], -turn) for turn in range(1, QUAD)]
    dkv = exchange(dkv.reshape(flat), ("head", "srv"))
    dkv, oqs = lax.optimization_barrier((dkv, oqs))
    dkv = call(
        fold_kernel,
        out_shape=(jax.ShapeDtypeStruct((part, wide), BF16),) * QUAD,
        in_specs=[vmem],
        out_specs=(vmem,) * QUAD,
        scratch_shapes=[
            pltpu.VMEM((GROUPS, BLOCKS * PIECE, wide), F32),
            pltpu.VMEM((BLOCKS, part, wide), F32),
        ],
        name="fold",
    )(dkv.reshape(slabs_shape))
    dkv = [carry_on(dkv[turn], turn) for turn in (2, 1, 3)] + [dkv[0]]
    k_grad, v_grad = call(
        finish_kernel,
        out_shape=(jax.ShapeDtypeStruct((PIECE, GROUPS * HEAD), BF16),) * 2,
        in_specs=[vmem] * QUAD,
        out_specs=(vmem, vmem),
        scratch_shapes=[pltpu.VMEM((part, wide), F32)],
        name="finish",
    )(*dkv)

    oq = sum(x.astype(F32) for x in oqs).astype(BF16)
    attention = oq[:, :HEAD].reshape(queries.shape)
    q_grad = oq[:, HEAD:].reshape(queries.shape)
    return attention, q_grad, k_grad, v_grad


def solution(mesh):
    placed = (
        P("dp", "srv", "head"),
        P(("dp", "head"), None),
        P(("dp", "head"), None),
        P("dp", "srv", "head"),
        P("dp"),
    )
    return jax.shard_map(
        local,
        mesh=mesh,
        in_specs=placed,
        out_specs=(
            P("dp", "srv", "head"),
            P("dp", "srv", "head"),
            P(("dp", "head", "srv"), None),
            P(("dp", "head", "srv"), None),
        ),
        check_vma=False,
    )
```

```python
import functools

import jax
import jax.numpy as jnp
from jax import lax
from jax.experimental import pallas as pl
from jax.experimental.pallas import tpu as pltpu
from jax.sharding import PartitionSpec as P

HEAD = 128
DP = 16
QUAD = 4
BLOCKS = 3
SHARD = 640
CONTEXT = 8192
ROWS = 512
DOC_MAX = 5120
DOCS = 8
GROUPS = 8
SRVS = 4
PIECE = SHARD // GROUPS // SRVS
SCALE = HEAD**-0.5
EXP2_SCALE = SCALE * 1.4426950408889634
NEGATIVE = -1e30
NEAR = tuple(tuple(range(QUAD * q, QUAD * q + QUAD)) for q in range(DP // QUAD))
FAR = tuple(tuple(range(m, DP, QUAD)) for m in range(QUAD))

F32 = jnp.float32
BF16 = jnp.bfloat16
NT = (((1,), (1,)), ((), ()))
NN = (((1,), (0,)), ((), ()))


def dot(lhs, rhs, dims):
    return lax.dot_general(lhs, rhs, dims, preferred_element_type=F32)


def flip(block):
    size = block.shape[1]
    rows = lax.broadcasted_iota(jnp.int32, (size, size), 0)
    columns = lax.broadcasted_iota(jnp.int32, (size, size), 1)
    return dot((rows == columns).astype(BF16), block, NT)


def fold8(block, op):
    rows, cols = block.shape
    return op(block.reshape(rows // 8, 8, cols), axis=0)


def member_of(member, turn):
    return member ^ turn


def fetch(sources, targets, sems):
    copies = [
        pltpu.make_async_copy(source, target, sems.at[i])
        for i, (source, target) in enumerate(zip(sources, targets))
    ]
    for copy in copies:
        copy.start()
    return copies


def pack_kernel(
    docs_in, keys_in, values_in, out_ref, docs, keys, values, k_ref, v_ref, f_ref, sems
):
    srv = lax.axis_index("srv")
    for copy in fetch((docs_in, keys_in, values_in), (docs, keys, values), sems):
        copy.wait()
    k_ref[...] = keys[...].astype(F32)
    v_ref[...] = values[...].astype(F32)

    def mine(ref):
        piece = ref[:PIECE, :]
        for part in range(1, SRVS):
            other = ref[PIECE * part : PIECE * (part + 1), :]
            piece = jnp.where(srv == part, other, piece)
        return piece

    k, v = mine(k_ref), mine(v_ref)
    for group in range(GROUPS):
        span = slice(PIECE * group, PIECE * (group + 1))
        columns = slice(HEAD * group, HEAD * (group + 1))
        f_ref[span, :HEAD] = k[:, columns]
        f_ref[span, HEAD:] = v[:, columns]
    lanes = lax.broadcasted_iota(jnp.int32, (8, 2 * HEAD), 1)
    row = jnp.zeros((8, 2 * HEAD), F32)
    for doc in range(DOCS):
        count = jnp.sum(jnp.where(docs[...] == doc, 1.0, 0.0), axis=1, keepdims=True)
        count = jnp.sum(count, axis=0, keepdims=True).astype(jnp.int32)
        row = jnp.where(lanes == doc, (count >> 6).astype(F32), row)
        row = jnp.where(lanes == DOCS + doc, (count & 63).astype(F32), row)
    first = lax.broadcasted_iota(jnp.int32, (8, 2 * HEAD), 0) == 0
    f_ref[PIECE * GROUPS :, :] = jnp.where(first, row, 0.0)
    out_ref[...] = f_ref[...].astype(BF16)


def join_kernel(packed, queries, gradient, own_ref, qg_ref):
    own_ref[...] = packed[...].astype(F32)
    qg_ref[:, :HEAD] = queries[...]
    qg_ref[:, HEAD:] = gradient[...]


def fan_kernel(p0, p1, p2, p3, joined, out_ref, qg_ref, f_ref, slab_ref):
    rows = joined.shape[0]
    dp = lax.axis_index("dp")
    quad, member = dp // QUAD, dp % QUAD
    for turn, part in enumerate((p0, p1, p2, p3)):
        f_ref[quad ^ turn] = part[...].astype(F32)
    for group in range(GROUPS):
        for block in range(BLOCKS):
            slab_ref[group, PIECE * block : PIECE * (block + 1), :] = f_ref[
                block + 1, PIECE * group : PIECE * (group + 1), :
            ]
        slab = slab_ref[group].astype(BF16)
        for srv in range(SRVS):
            out_ref[group, srv] = slab
    count = jnp.zeros((8, 2 * HEAD), F32)
    for owner in range(1, QUAD):
        held = f_ref[owner, PIECE * GROUPS :, :]
        count += jnp.where(reached(quad, QUAD * owner + member), held, 0.0)
    qg_ref[:rows, :] = joined[...]
    qg_ref[rows:, :] = count.astype(BF16)


def fold_kernel(parts, own_ref, next_ref, far_ref, last_ref, slab_ref, f_ref):
    quad = lax.axis_index("dp") // QUAD
    for group in range(GROUPS):
        slab_ref[group] = sum(parts[group, srv].astype(F32) for srv in range(SRVS))
        for block in range(BLOCKS):
            f_ref[block, PIECE * group : PIECE * (group + 1), :] = slab_ref[
                group, PIECE * block : PIECE * (block + 1), :
            ]
    for turn, ref in enumerate((own_ref, next_ref, far_ref, last_ref)):
        owner = quad ^ turn
        ref[...] = f_ref[jnp.maximum(owner - 1, 0)].astype(BF16)

    @pl.when(quad == 0)
    def _():
        own_ref[...] = jnp.zeros(own_ref.shape, BF16)


def finish_kernel(p0, p1, p2, p3, k_ref, v_ref, f_ref):
    f_ref[...] = sum(part[...].astype(F32) for part in (p0, p1, p2, p3))
    for group in range(GROUPS):
        span = slice(PIECE * group, PIECE * (group + 1))
        columns = slice(HEAD * group, HEAD * (group + 1))
        k_ref[:, columns] = f_ref[span, :HEAD].astype(BF16)
        v_ref[:, columns] = f_ref[span, HEAD:].astype(BF16)


def forward_kernel(
    qg, slabs, e_ref, o_ref, stats_ref, active, kv, s_ref, m_ref, l_ref, slab_ref, f_ref
):
    dp = lax.axis_index("dp")
    quad, member = dp // QUAD, dp % QUAD
    qs = [qg.at[member_of(member, turn)] for turn in range(QUAD)]
    cols = o_ref.shape[2]
    keys = kv.shape[1]
    query_at = CONTEXT + 2 * cols * quad

    window_end = ((query_at + ROWS - 1) // SHARD + 1) * SHARD
    count = sum(jnp.sum(qg[who, cols:, :].astype(F32), axis=0, keepdims=True) for who in range(QUAD))
    lanes = lax.broadcasted_iota(jnp.int32, count.shape, 1)
    starts = []
    for doc in range(DOCS):
        high = jnp.sum(jnp.where((lanes >= doc) & (lanes < DOCS), count, 0.0)) * 64.0
        low = jnp.sum(
            jnp.where((lanes >= DOCS + doc) & (lanes < 2 * DOCS), count, 0.0)
        )
        starts.append(window_end - (high + low).astype(jnp.int32))
    reach = jnp.int32(0)
    for start in starts:
        reach = jnp.where(start <= query_at, jnp.maximum(reach, start), reach)
    first, last = jnp.int32(0), jnp.int32(0)
    for block in range(BLOCKS):
        shard = SHARD * (QUAD * (block + 1) + member)
        first += (shard + SHARD <= reach).astype(jnp.int32)
        last += (shard < query_at + 2 * cols).astype(jnp.int32)
    active[0] = first
    active[1] = last

    for group in range(GROUPS):
        for srv in range(SRVS):
            slab_ref[group, srv] = slabs[group, srv].astype(F32)
            at = PIECE * (SRVS * group + srv)
            for block in range(BLOCKS):
                f_ref[block, at : at + PIECE, :] = slab_ref[
                    group, srv, PIECE * block : PIECE * (block + 1), :
                ]
    for block in range(BLOCKS):
        kv[block] = f_ref[block].astype(BF16)

    pattern = lax.broadcasted_iota(jnp.int32, (keys, cols), 0) + SHARD * (QUAD + member)
    lane = lax.broadcasted_iota(jnp.int32, (1, cols), 1)
    m_ref[...] = jnp.full(m_ref.shape, NEGATIVE, F32)
    l_ref[...] = jnp.zeros(l_ref.shape, F32)
    o_ref[...] = jnp.zeros(o_ref.shape, F32)
    query_places, doc_starts = [], []
    for turn in range(QUAD):
        query_place = query_at + (cols // 2) * member_of(member, turn) + lane // 2
        doc_start = jnp.zeros_like(query_place)
        for start in starts:
            doc_start = jnp.where(start <= query_place, jnp.maximum(doc_start, start), doc_start)
        query_places.append(query_place)
        doc_starts.append(doc_start)

    def scores(t, carry):
        k = kv[t, :, :HEAD]
        key_place = pattern + QUAD * SHARD * t
        for turn in range(QUAD):
            span = pl.ds(turn * cols, cols)
            s = dot(k, qs[turn][:cols, :HEAD], NT)
            allowed = (key_place >= doc_starts[turn]) & (key_place <= query_places[turn])
            s = jnp.where(allowed, s, NEGATIVE)
            s_ref[t, :, span] = s
            m_ref[turn] = jnp.maximum(m_ref[turn], fold8(s, jnp.max))
        return carry

    lax.fori_loop(first, last, scores, 0)
    tops = [jnp.max(m_ref[turn], axis=0, keepdims=True) for turn in range(QUAD)]

    def weigh(t, carry):
        v = flip(kv[t, :, HEAD:]).astype(BF16)
        for turn in range(QUAD):
            span = pl.ds(turn * cols, cols)
            e = jnp.exp2((s_ref[t, :, span] - tops[turn]) * EXP2_SCALE)
            l_ref[turn] += fold8(e, jnp.sum)
            e = e.astype(BF16)
            e_ref[t, :, span] = e
            o_ref[turn] += dot(v, e, NN)
        return carry

    lax.fori_loop(first, last, weigh, 0)
    for turn in range(QUAD):
        tile = member_of(member, turn)
        gradient = flip(qs[turn][:cols, HEAD:])
        norm = jnp.sum(l_ref[turn], axis=0, keepdims=True)
        delta = jnp.sum(gradient * o_ref[turn], axis=0, keepdims=True)
        for copy in range(QUAD):
            stats_ref[copy, pl.ds(tile, 1), :] = tops[turn]
            stats_ref[copy, pl.ds(QUAD + tile, 1), :] = norm
            stats_ref[copy, pl.ds(2 * QUAD + tile, 1), :] = delta
            stats_ref[copy, pl.ds(3 * QUAD + tile, 1), :] = jnp.zeros_like(norm)


def backward_kernel(
    active, qg, kv, e_ref, o_ref, stats, oq0, oq1, oq2, oq3, dkv_ref, dq_ref, f_ref, slab_ref
):
    member = lax.axis_index("dp") % QUAD
    first, last = active[0], active[1]
    qs = [qg.at[member_of(member, turn)] for turn in range(QUAD)]
    oqs = (oq0, oq1, oq2, oq3)
    cols = o_ref.shape[2]
    keys = kv.shape[1]
    dq_ref[...] = jnp.zeros(dq_ref.shape, F32)
    shares, deltas = [], []
    for turn in range(QUAD):
        tile = member_of(member, turn)
        row = lambda who, kind: stats[who, pl.ds(kind * QUAD + tile, 1), :]
        top = functools.reduce(jnp.maximum, [row(who, 0) for who in range(QUAD)])
        weights = [jnp.exp2((row(who, 0) - top) * EXP2_SCALE) for who in range(QUAD)]
        norm = sum(weights[who] * row(who, 1) for who in range(QUAD))
        deltas.append(sum(weights[who] * row(who, 2) for who in range(QUAD)) / norm)
        shares.append(jnp.exp2((row(member, 0) - top) * EXP2_SCALE) / norm)

    def clear(t, carry):
        f_ref[t] = jnp.zeros((keys, 2 * HEAD), F32)
        return carry

    lax.fori_loop(0, first, clear, 0)
    lax.fori_loop(last, BLOCKS, clear, 0)

    def grads(t, carry):
        k = kv[t, :, :HEAD]
        v = kv[t, :, HEAD:]
        kt = flip(k).astype(BF16)
        dk = jnp.zeros((keys, HEAD), F32)
        dv = jnp.zeros((keys, HEAD), F32)
        for turn in range(QUAD):
            q, gradient = qs[turn][:cols, :HEAD], qs[turn][:cols, HEAD:]
            p = e_ref[t, :, pl.ds(turn * cols, cols)].astype(F32) * shares[turn]
            ds = (p * (dot(v, gradient, NT) - deltas[turn])).astype(BF16)
            dv += dot(p.astype(BF16), gradient, NN)
            dk += dot(ds, q, NN)
            dq_ref[turn] += dot(kt, ds, NN)
        f_ref[t, :, :HEAD] = dk * SCALE
        f_ref[t, :, HEAD:] = dv
        return carry

    lax.fori_loop(first, last, grads, 0)
    for turn in range(QUAD):
        oqs[turn][:, :HEAD] = flip((o_ref[turn] * shares[turn]).astype(BF16)).astype(BF16)
        oqs[turn][:, HEAD:] = flip((dq_ref[turn] * SCALE).astype(BF16)).astype(BF16)
    for group in range(GROUPS):
        for srv in range(SRVS):
            at = PIECE * (SRVS * group + srv)
            for block in range(BLOCKS):
                slab_ref[group, srv, PIECE * block : PIECE * (block + 1), :] = f_ref[
                    block, at : at + PIECE, :
                ]
            dkv_ref[group, srv] = slab_ref[group, srv].astype(BF16)


def exchange(block, axis, groups=None):
    return lax.all_to_all(block, axis, 0, 0, tiled=True, axis_index_groups=groups)


def swap(block, turn):
    return lax.ppermute(block, "dp", [(place, place ^ turn) for place in range(DP)])


def reached(quad, shard):
    first = CONTEXT + ROWS * quad
    return (first - (DOC_MAX - 1) < SHARD * (shard + 1)) & (SHARD * shard < first + ROWS)


def hand_out(block, turn):
    pairs = []
    for owner in range(1, QUAD):
        quad = owner ^ turn
        for m in range(QUAD):
            if reached(quad, QUAD * owner + m):
                pairs.append((QUAD * owner + m, QUAD * quad + m))
    return lax.ppermute(block, "dp", pairs)


def carry_on(block, turn):
    pairs = []
    for quad in range(QUAD):
        owner = quad ^ turn
        for m in range(QUAD) if owner else ():
            if reached(quad, QUAD * owner + m):
                pairs.append((QUAD * quad + m, QUAD * owner + m))
    return lax.ppermute(block, "dp", pairs)


def local(queries, keys, values, output_gradient, doc_ids):
    rows = queries.shape[0] * queries.shape[1]
    part = GROUPS * PIECE
    wide = 2 * HEAD
    vmem = pl.BlockSpec(memory_space=pltpu.VMEM)
    smem = pl.BlockSpec(memory_space=pltpu.SMEM)
    params = pltpu.CompilerParams(vmem_limit_bytes=30 * 1024 * 1024)
    roomy = pltpu.CompilerParams(vmem_limit_bytes=60 * 1024 * 1024)
    call = functools.partial(pl.pallas_call, compiler_params=params)
    slabs_shape = (GROUPS, SRVS, BLOCKS * PIECE, wide)

    hbm = pl.BlockSpec(memory_space=pltpu.HBM)
    sources = (doc_ids.reshape(-1, 128), keys, values)
    packed = pl.pallas_call(
        pack_kernel,
        out_shape=jax.ShapeDtypeStruct((part + 8, wide), BF16),
        in_specs=[hbm] * 3,
        out_specs=vmem,
        scratch_shapes=[pltpu.VMEM(x.shape, x.dtype) for x in sources]
        + [
            pltpu.VMEM(keys.shape, F32),
            pltpu.VMEM(values.shape, F32),
            pltpu.VMEM((part + 8, wide), F32),
            pltpu.SemaphoreType.DMA((3,)),
        ],
        compiler_params=roomy,
        name="pack",
    )(*sources)
    parts = [hand_out(packed, turn) for turn in (2, 3, 1)]
    own, joined = call(
        join_kernel,
        out_shape=(
            jax.ShapeDtypeStruct((part + 8, wide), F32),
            jax.ShapeDtypeStruct((rows, wide), BF16),
        ),
        in_specs=[vmem] * 3,
        out_specs=(vmem, vmem),
        name="join",
    )(packed, queries.reshape(rows, HEAD), output_gradient.reshape(rows, HEAD))
    slabs, qg = pl.pallas_call(
        fan_kernel,
        out_shape=(
            jax.ShapeDtypeStruct(slabs_shape, BF16),
            jax.ShapeDtypeStruct((rows + 8, wide), BF16),
        ),
        in_specs=[vmem] * (QUAD + 1),
        out_specs=(vmem, vmem),
        scratch_shapes=[
            pltpu.VMEM((QUAD, part + 8, wide), F32),
            pltpu.VMEM((GROUPS, BLOCKS * PIECE, wide), F32),
        ],
        compiler_params=params,
        name="fan",
    )(own, parts[2], parts[0], parts[1], joined)
    flat = (GROUPS * SRVS, BLOCKS * PIECE, wide)
    slabs = exchange(slabs.reshape(flat), ("head", "srv")).reshape(slabs_shape)
    qg = lax.all_gather(qg, "dp", axis=0, axis_index_groups=NEAR)

    e, o, stats, active, kv = call(
        forward_kernel,
        out_shape=(
            jax.ShapeDtypeStruct((BLOCKS, SHARD, QUAD * rows), BF16),
            jax.ShapeDtypeStruct((QUAD, HEAD, rows), F32),
            jax.ShapeDtypeStruct((QUAD, 4 * QUAD, rows), F32),
            jax.ShapeDtypeStruct((2,), jnp.int32),
            jax.ShapeDtypeStruct((BLOCKS, SHARD, wide), BF16),
        ),
        in_specs=[vmem] * 2,
        out_specs=(vmem, vmem, vmem, smem, vmem),
        scratch_shapes=[
            pltpu.VMEM((BLOCKS, SHARD, QUAD * rows), F32),
            pltpu.VMEM((QUAD, 8, rows), F32),
            pltpu.VMEM((QUAD, 8, rows), F32),
            pltpu.VMEM(slabs_shape, F32),
            pltpu.VMEM((BLOCKS, SHARD, wide), F32),
        ],
        name="forward",
    )(qg, slabs)
    stats = exchange(stats.reshape(QUAD * 4 * QUAD, rows), "dp", NEAR)
    stats = stats.reshape(QUAD, 4 * QUAD, rows)
    *oqs, dkv = call(
        backward_kernel,
        out_shape=(
            *[jax.ShapeDtypeStruct((rows, wide), BF16)] * QUAD,
            jax.ShapeDtypeStruct(slabs_shape, BF16),
        ),
        in_specs=[smem] + [vmem] * 5,
        out_specs=(vmem,) * 5,
        scratch_shapes=[
            pltpu.VMEM((QUAD, HEAD, rows), F32),
            pltpu.VMEM((BLOCKS, SHARD, wide), F32),
            pltpu.VMEM(slabs_shape, F32),
        ],
        name="backward",
    )(active, qg, kv, e, o, stats)

    oqs = [swap(oqs[turn], turn) for turn in (3, 2, 1)] + [oqs[0]]
    dkv = exchange(dkv.reshape(flat), ("head", "srv"))
    dkv, oqs = lax.optimization_barrier((dkv, oqs))
    dkv = call(
        fold_kernel,
        out_shape=(jax.ShapeDtypeStruct((part, wide), BF16),) * QUAD,
        in_specs=[vmem],
        out_specs=(vmem,) * QUAD,
        scratch_shapes=[
            pltpu.VMEM((GROUPS, BLOCKS * PIECE, wide), F32),
            pltpu.VMEM((BLOCKS, part, wide), F32),
        ],
        name="fold",
    )(dkv.reshape(slabs_shape))
    dkv = [carry_on(dkv[turn], turn) for turn in (2, 3, 1)] + [dkv[0]]
    k_grad, v_grad = call(
        finish_kernel,
        out_shape=(jax.ShapeDtypeStruct((PIECE, GROUPS * HEAD), BF16),) * 2,
        in_specs=[vmem] * QUAD,
        out_specs=(vmem, vmem),
        scratch_shapes=[pltpu.VMEM((part, wide), F32)],
        name="finish",
    )(*dkv)

    oq = sum(x.astype(F32) for x in oqs).astype(BF16)
    attention = oq[:, :HEAD].reshape(queries.shape)
    q_grad = oq[:, HEAD:].reshape(queries.shape)
    return attention, q_grad, k_grad, v_grad


def solution(mesh):
    placed = (
        P("dp", "srv", "head"),
        P(("dp", "head"), None),
        P(("dp", "head"), None),
        P("dp", "srv", "head"),
        P("dp"),
    )
    return jax.shard_map(
        local,
        mesh=mesh,
        in_specs=placed,
        out_specs=(
            P("dp", "srv", "head"),
            P("dp", "srv", "head"),
            P(("dp", "head", "srv"), None),
            P(("dp", "head", "srv"), None),
        ),
        check_vma=False,
    )
```

```python
import functools

import jax
import jax.numpy as jnp
from jax import lax
from jax.experimental import pallas as pl
from jax.experimental.pallas import tpu as pltpu
from jax.sharding import PartitionSpec as P

HEAD = 128
DP = 16
QUAD = 4
BLOCKS = 3
SHARD = 640
CONTEXT = 8192
ROWS = 512
DOC_MAX = 5120
DOCS = 8
GROUPS = 8
SRVS = 4
PIECE = SHARD // GROUPS // SRVS
SCALE = HEAD**-0.5
EXP2_SCALE = SCALE * 1.4426950408889634
NEGATIVE = -1e30
NEAR = tuple(tuple(range(QUAD * q, QUAD * q + QUAD)) for q in range(DP // QUAD))
FAR = tuple(tuple(range(m, DP, QUAD)) for m in range(QUAD))

F32 = jnp.float32
BF16 = jnp.bfloat16
NT = (((1,), (1,)), ((), ()))
NN = (((1,), (0,)), ((), ()))


def dot(lhs, rhs, dims):
    return lax.dot_general(lhs, rhs, dims, preferred_element_type=F32)


def flip(block):
    size = block.shape[1]
    rows = lax.broadcasted_iota(jnp.int32, (size, size), 0)
    columns = lax.broadcasted_iota(jnp.int32, (size, size), 1)
    return dot((rows == columns).astype(BF16), block, NT)


def fold8(block, op):
    rows, cols = block.shape
    return op(block.reshape(rows // 8, 8, cols), axis=0)


def member_of(member, turn):
    return member ^ turn


def fetch(sources, targets, sems):
    copies = [
        pltpu.make_async_copy(source, target, sems.at[i])
        for i, (source, target) in enumerate(zip(sources, targets))
    ]
    for copy in copies:
        copy.start()
    return copies


def pack_kernel(
    docs_in, keys_in, values_in, out_ref, docs, keys, values, k_ref, v_ref, f_ref, sems
):
    srv = lax.axis_index("srv")
    for copy in fetch((docs_in, keys_in, values_in), (docs, keys, values), sems):
        copy.wait()
    k_ref[...] = keys[...].astype(F32)
    v_ref[...] = values[...].astype(F32)

    def mine(ref):
        piece = ref[:PIECE, :]
        for part in range(1, SRVS):
            other = ref[PIECE * part : PIECE * (part + 1), :]
            piece = jnp.where(srv == part, other, piece)
        return piece

    k, v = mine(k_ref), mine(v_ref)
    for group in range(GROUPS):
        span = slice(PIECE * group, PIECE * (group + 1))
        columns = slice(HEAD * group, HEAD * (group + 1))
        f_ref[span, :HEAD] = k[:, columns]
        f_ref[span, HEAD:] = v[:, columns]
    lanes = lax.broadcasted_iota(jnp.int32, (8, 2 * HEAD), 1)
    row = jnp.zeros((8, 2 * HEAD), F32)
    for doc in range(DOCS):
        count = jnp.sum(jnp.where(docs[...] == doc, 1.0, 0.0), axis=1, keepdims=True)
        count = jnp.sum(count, axis=0, keepdims=True).astype(jnp.int32)
        row = jnp.where(lanes == doc, (count >> 6).astype(F32), row)
        row = jnp.where(lanes == DOCS + doc, (count & 63).astype(F32), row)
    first = lax.broadcasted_iota(jnp.int32, (8, 2 * HEAD), 0) == 0
    f_ref[PIECE * GROUPS :, :] = jnp.where(first, row, 0.0)
    out_ref[...] = f_ref[...].astype(BF16)


def join_kernel(packed, queries, gradient, own_ref, qg_ref):
    own_ref[...] = packed[...].astype(F32)
    qg_ref[:, :HEAD] = queries[...]
    qg_ref[:, HEAD:] = gradient[...]


def fan_kernel(p0, p1, p2, p3, joined, out_ref, qg_ref, f_ref, slab_ref):
    rows = joined.shape[0]
    dp = lax.axis_index("dp")
    quad, member = dp // QUAD, dp % QUAD
    for turn, part in enumerate((p0, p1, p2, p3)):
        f_ref[quad ^ turn] = part[...].astype(F32)
    for group in range(GROUPS):
        for block in range(BLOCKS):
            slab_ref[group, PIECE * block : PIECE * (block + 1), :] = f_ref[
                block + 1, PIECE * group : PIECE * (group + 1), :
            ]
        slab = slab_ref[group].astype(BF16)
        for srv in range(SRVS):
            out_ref[group, srv] = slab
    count = jnp.zeros((8, 2 * HEAD), F32)
    for owner in range(1, QUAD):
        held = f_ref[owner, PIECE * GROUPS :, :]
        count += jnp.where(reached(quad, QUAD * owner + member), held, 0.0)
    qg_ref[:rows, :] = joined[...]
    qg_ref[rows:, :] = count.astype(BF16)


def fold_kernel(parts, own_ref, next_ref, far_ref, last_ref, slab_ref, f_ref):
    quad = lax.axis_index("dp") // QUAD
    for group in range(GROUPS):
        slab_ref[group] = sum(parts[group, srv].astype(F32) for srv in range(SRVS))
        for block in range(BLOCKS):
            f_ref[block, PIECE * group : PIECE * (group + 1), :] = slab_ref[
                group, PIECE * block : PIECE * (block + 1), :
            ]
    for turn, ref in enumerate((own_ref, next_ref, far_ref, last_ref)):
        owner = quad ^ turn
        ref[...] = f_ref[jnp.maximum(owner - 1, 0)].astype(BF16)

    @pl.when(quad == 0)
    def _():
        own_ref[...] = jnp.zeros(own_ref.shape, BF16)


def finish_kernel(p0, p1, p2, p3, k_ref, v_ref, f_ref):
    f_ref[...] = sum(part[...].astype(F32) for part in (p0, p1, p2, p3))
    for group in range(GROUPS):
        span = slice(PIECE * group, PIECE * (group + 1))
        columns = slice(HEAD * group, HEAD * (group + 1))
        k_ref[:, columns] = f_ref[span, :HEAD].astype(BF16)
        v_ref[:, columns] = f_ref[span, HEAD:].astype(BF16)


def forward_kernel(
    qg, slabs, e_ref, o_ref, stats_ref, active, kv, s_ref, m_ref, l_ref, slab_ref, f_ref
):
    dp = lax.axis_index("dp")
    quad, member = dp // QUAD, dp % QUAD
    qs = [qg.at[member_of(member, turn)] for turn in range(QUAD)]
    cols = o_ref.shape[2]
    keys = kv.shape[1]
    query_at = CONTEXT + 2 * cols * quad

    window_end = ((query_at + ROWS - 1) // SHARD + 1) * SHARD
    count = sum(jnp.sum(qg[who, cols:, :].astype(F32), axis=0, keepdims=True) for who in range(QUAD))
    lanes = lax.broadcasted_iota(jnp.int32, count.shape, 1)
    starts = []
    for doc in range(DOCS):
        high = jnp.sum(jnp.where((lanes >= doc) & (lanes < DOCS), count, 0.0)) * 64.0
        low = jnp.sum(
            jnp.where((lanes >= DOCS + doc) & (lanes < 2 * DOCS), count, 0.0)
        )
        starts.append(window_end - (high + low).astype(jnp.int32))
    reach = jnp.int32(0)
    for start in starts:
        reach = jnp.where(start <= query_at, jnp.maximum(reach, start), reach)
    first, last = jnp.int32(0), jnp.int32(0)
    for block in range(BLOCKS):
        shard = SHARD * (QUAD * (block + 1) + member)
        first += (shard + SHARD <= reach).astype(jnp.int32)
        last += (shard < query_at + 2 * cols).astype(jnp.int32)
    active[0] = first
    active[1] = last

    for group in range(GROUPS):
        for srv in range(SRVS):
            slab_ref[group, srv] = slabs[group, srv].astype(F32)
            at = PIECE * (SRVS * group + srv)
            for block in range(BLOCKS):
                f_ref[block, at : at + PIECE, :] = slab_ref[
                    group, srv, PIECE * block : PIECE * (block + 1), :
                ]
    for block in range(BLOCKS):
        kv[block] = f_ref[block].astype(BF16)

    pattern = lax.broadcasted_iota(jnp.int32, (keys, cols), 0) + SHARD * (QUAD + member)
    lane = lax.broadcasted_iota(jnp.int32, (1, cols), 1)
    m_ref[...] = jnp.full(m_ref.shape, NEGATIVE, F32)
    l_ref[...] = jnp.zeros(l_ref.shape, F32)
    o_ref[...] = jnp.zeros(o_ref.shape, F32)
    query_places, doc_starts = [], []
    for turn in range(QUAD):
        query_place = query_at + (cols // 2) * member_of(member, turn) + lane // 2
        doc_start = jnp.zeros_like(query_place)
        for start in starts:
            doc_start = jnp.where(start <= query_place, jnp.maximum(doc_start, start), doc_start)
        query_places.append(query_place)
        doc_starts.append(doc_start)

    def scores(t, carry):
        k = kv[t, :, :HEAD]
        key_place = pattern + QUAD * SHARD * t
        for turn in range(QUAD):
            span = pl.ds(turn * cols, cols)
            s = dot(k, qs[turn][:cols, :HEAD], NT)
            allowed = (key_place >= doc_starts[turn]) & (key_place <= query_places[turn])
            s = jnp.where(allowed, s, NEGATIVE)
            s_ref[t, :, span] = s
            m_ref[turn] = jnp.maximum(m_ref[turn], fold8(s, jnp.max))
        return carry

    lax.fori_loop(first, last, scores, 0)
    tops = [jnp.max(m_ref[turn], axis=0, keepdims=True) for turn in range(QUAD)]

    def weigh(t, carry):
        v = flip(kv[t, :, HEAD:]).astype(BF16)
        for turn in range(QUAD):
            span = pl.ds(turn * cols, cols)
            e = jnp.exp2((s_ref[t, :, span] - tops[turn]) * EXP2_SCALE)
            l_ref[turn] += fold8(e, jnp.sum)
            e = e.astype(BF16)
            e_ref[t, :, span] = e
            o_ref[turn] += dot(v, e, NN)
        return carry

    lax.fori_loop(first, last, weigh, 0)
    for turn in range(QUAD):
        tile = member_of(member, turn)
        gradient = flip(qs[turn][:cols, HEAD:])
        norm = jnp.sum(l_ref[turn], axis=0, keepdims=True)
        delta = jnp.sum(gradient * o_ref[turn], axis=0, keepdims=True)
        for copy in range(QUAD):
            stats_ref[copy, pl.ds(tile, 1), :] = tops[turn]
            stats_ref[copy, pl.ds(QUAD + tile, 1), :] = norm
            stats_ref[copy, pl.ds(2 * QUAD + tile, 1), :] = delta
            stats_ref[copy, pl.ds(3 * QUAD + tile, 1), :] = jnp.zeros_like(norm)


def backward_kernel(
    active, qg, kv, e_ref, o_ref, stats, oq0, oq1, oq2, oq3, dkv_ref, dq_ref, f_ref, slab_ref
):
    member = lax.axis_index("dp") % QUAD
    first, last = active[0], active[1]
    qs = [qg.at[member_of(member, turn)] for turn in range(QUAD)]
    oqs = (oq0, oq1, oq2, oq3)
    cols = o_ref.shape[2]
    keys = kv.shape[1]
    dq_ref[...] = jnp.zeros(dq_ref.shape, F32)
    shares, deltas = [], []
    for turn in range(QUAD):
        tile = member_of(member, turn)
        row = lambda who, kind: stats[who, pl.ds(kind * QUAD + tile, 1), :]
        top = functools.reduce(jnp.maximum, [row(who, 0) for who in range(QUAD)])
        weights = [jnp.exp2((row(who, 0) - top) * EXP2_SCALE) for who in range(QUAD)]
        norm = sum(weights[who] * row(who, 1) for who in range(QUAD))
        deltas.append(sum(weights[who] * row(who, 2) for who in range(QUAD)) / norm)
        shares.append(jnp.exp2((row(member, 0) - top) * EXP2_SCALE) / norm)

    def clear(t, carry):
        f_ref[t] = jnp.zeros((keys, 2 * HEAD), F32)
        return carry

    lax.fori_loop(0, first, clear, 0)
    lax.fori_loop(last, BLOCKS, clear, 0)

    def grads(t, carry):
        k = kv[t, :, :HEAD]
        v = kv[t, :, HEAD:]
        kt = flip(k).astype(BF16)
        dk = jnp.zeros((keys, HEAD), F32)
        dv = jnp.zeros((keys, HEAD), F32)
        for turn in range(QUAD):
            q, gradient = qs[turn][:cols, :HEAD], qs[turn][:cols, HEAD:]
            p = e_ref[t, :, pl.ds(turn * cols, cols)].astype(F32) * shares[turn]
            ds = (p * (dot(v, gradient, NT) - deltas[turn])).astype(BF16)
            dv += dot(p.astype(BF16), gradient, NN)
            dk += dot(ds, q, NN)
            dq_ref[turn] += dot(kt, ds, NN)
        f_ref[t, :, :HEAD] = dk * SCALE
        f_ref[t, :, HEAD:] = dv
        return carry

    lax.fori_loop(first, last, grads, 0)
    for turn in range(QUAD):
        oqs[turn][:, :HEAD] = flip((o_ref[turn] * shares[turn]).astype(BF16)).astype(BF16)
        oqs[turn][:, HEAD:] = flip((dq_ref[turn] * SCALE).astype(BF16)).astype(BF16)
    for group in range(GROUPS):
        for srv in range(SRVS):
            at = PIECE * (SRVS * group + srv)
            for block in range(BLOCKS):
                slab_ref[group, srv, PIECE * block : PIECE * (block + 1), :] = f_ref[
                    block, at : at + PIECE, :
                ]
            dkv_ref[group, srv] = slab_ref[group, srv].astype(BF16)


def exchange(block, axis, groups=None):
    return lax.all_to_all(block, axis, 0, 0, tiled=True, axis_index_groups=groups)


def swap(block, turn):
    return lax.ppermute(block, "dp", [(place, place ^ turn) for place in range(DP)])


def reached(quad, shard):
    first = CONTEXT + ROWS * quad
    return (first - (DOC_MAX - 1) < SHARD * (shard + 1)) & (SHARD * shard < first + ROWS)


def hand_out(block, turn):
    pairs = []
    for owner in range(1, QUAD):
        quad = owner ^ turn
        for m in range(QUAD):
            if reached(quad, QUAD * owner + m):
                pairs.append((QUAD * owner + m, QUAD * quad + m))
    return lax.ppermute(block, "dp", pairs)


def carry_on(block, turn):
    pairs = []
    for quad in range(QUAD):
        owner = quad ^ turn
        for m in range(QUAD) if owner else ():
            if reached(quad, QUAD * owner + m):
                pairs.append((QUAD * quad + m, QUAD * owner + m))
    return lax.ppermute(block, "dp", pairs)


def local(queries, keys, values, output_gradient, doc_ids):
    rows = queries.shape[0] * queries.shape[1]
    part = GROUPS * PIECE
    wide = 2 * HEAD
    vmem = pl.BlockSpec(memory_space=pltpu.VMEM)
    smem = pl.BlockSpec(memory_space=pltpu.SMEM)
    params = pltpu.CompilerParams(vmem_limit_bytes=30 * 1024 * 1024)
    roomy = pltpu.CompilerParams(vmem_limit_bytes=60 * 1024 * 1024)
    call = functools.partial(pl.pallas_call, compiler_params=params)
    slabs_shape = (GROUPS, SRVS, BLOCKS * PIECE, wide)

    hbm = pl.BlockSpec(memory_space=pltpu.HBM)
    sources = (doc_ids.reshape(-1, 128), keys, values)
    packed = pl.pallas_call(
        pack_kernel,
        out_shape=jax.ShapeDtypeStruct((part + 8, wide), BF16),
        in_specs=[hbm] * 3,
        out_specs=vmem,
        scratch_shapes=[pltpu.VMEM(x.shape, x.dtype) for x in sources]
        + [
            pltpu.VMEM(keys.shape, F32),
            pltpu.VMEM(values.shape, F32),
            pltpu.VMEM((part + 8, wide), F32),
            pltpu.SemaphoreType.DMA((3,)),
        ],
        compiler_params=roomy,
        name="pack",
    )(*sources)
    parts = [hand_out(packed, turn) for turn in (2, 3, 1)]
    own, joined = call(
        join_kernel,
        out_shape=(
            jax.ShapeDtypeStruct((part + 8, wide), F32),
            jax.ShapeDtypeStruct((rows, wide), BF16),
        ),
        in_specs=[vmem] * 3,
        out_specs=(vmem, vmem),
        name="join",
    )(packed, queries.reshape(rows, HEAD), output_gradient.reshape(rows, HEAD))
    slabs, qg = pl.pallas_call(
        fan_kernel,
        out_shape=(
            jax.ShapeDtypeStruct(slabs_shape, BF16),
            jax.ShapeDtypeStruct((rows + 8, wide), BF16),
        ),
        in_specs=[vmem] * (QUAD + 1),
        out_specs=(vmem, vmem),
        scratch_shapes=[
            pltpu.VMEM((QUAD, part + 8, wide), F32),
            pltpu.VMEM((GROUPS, BLOCKS * PIECE, wide), F32),
        ],
        compiler_params=params,
        name="fan",
    )(own, parts[2], parts[0], parts[1], joined)
    flat = (GROUPS * SRVS, BLOCKS * PIECE, wide)
    slabs = exchange(slabs.reshape(flat), ("head", "srv")).reshape(slabs_shape)
    qg = lax.all_gather(qg, "dp", axis=0, axis_index_groups=NEAR)

    e, o, stats, active, kv = call(
        forward_kernel,
        out_shape=(
            jax.ShapeDtypeStruct((BLOCKS, SHARD, QUAD * rows), BF16),
            jax.ShapeDtypeStruct((QUAD, HEAD, rows), F32),
            jax.ShapeDtypeStruct((QUAD, 4 * QUAD, rows), F32),
            jax.ShapeDtypeStruct((2,), jnp.int32),
            jax.ShapeDtypeStruct((BLOCKS, SHARD, wide), BF16),
        ),
        in_specs=[vmem] * 2,
        out_specs=(vmem, vmem, vmem, smem, vmem),
        scratch_shapes=[
            pltpu.VMEM((BLOCKS, SHARD, QUAD * rows), F32),
            pltpu.VMEM((QUAD, 8, rows), F32),
            pltpu.VMEM((QUAD, 8, rows), F32),
            pltpu.VMEM(slabs_shape, F32),
            pltpu.VMEM((BLOCKS, SHARD, wide), F32),
        ],
        name="forward",
    )(qg, slabs)
    stats = exchange(stats.reshape(QUAD * 4 * QUAD, rows), "dp", NEAR)
    stats = stats.reshape(QUAD, 4 * QUAD, rows)
    *oqs, dkv = call(
        backward_kernel,
        out_shape=(
            *[jax.ShapeDtypeStruct((rows, wide), BF16)] * QUAD,
            jax.ShapeDtypeStruct(slabs_shape, BF16),
        ),
        in_specs=[smem] + [vmem] * 5,
        out_specs=(vmem,) * 5,
        scratch_shapes=[
            pltpu.VMEM((QUAD, HEAD, rows), F32),
            pltpu.VMEM((BLOCKS, SHARD, wide), F32),
            pltpu.VMEM(slabs_shape, F32),
        ],
        name="backward",
    )(active, qg, kv, e, o, stats)

    oqs = [swap(oqs[turn], turn) for turn in (3, 2, 1)] + [oqs[0]]
    dkv = exchange(dkv.reshape(flat), ("head", "srv"))
    dkv = call(
        fold_kernel,
        out_shape=(jax.ShapeDtypeStruct((part, wide), BF16),) * QUAD,
        in_specs=[vmem],
        out_specs=(vmem,) * QUAD,
        scratch_shapes=[
            pltpu.VMEM((GROUPS, BLOCKS * PIECE, wide), F32),
            pltpu.VMEM((BLOCKS, part, wide), F32),
        ],
        name="fold",
    )(dkv.reshape(slabs_shape))
    dkv = [carry_on(dkv[turn], turn) for turn in (3, 2, 1)] + [dkv[0]]
    k_grad, v_grad = call(
        finish_kernel,
        out_shape=(jax.ShapeDtypeStruct((PIECE, GROUPS * HEAD), BF16),) * 2,
        in_specs=[vmem] * QUAD,
        out_specs=(vmem, vmem),
        scratch_shapes=[pltpu.VMEM((part, wide), F32)],
        name="finish",
    )(*dkv)

    oq = sum(x.astype(F32) for x in oqs).astype(BF16)
    attention = oq[:, :HEAD].reshape(queries.shape)
    q_grad = oq[:, HEAD:].reshape(queries.shape)
    return attention, q_grad, k_grad, v_grad


def solution(mesh):
    placed = (
        P("dp", "srv", "head"),
        P(("dp", "head"), None),
        P(("dp", "head"), None),
        P("dp", "srv", "head"),
        P("dp"),
    )
    return jax.shard_map(
        local,
        mesh=mesh,
        in_specs=placed,
        out_specs=(
            P("dp", "srv", "head"),
            P("dp", "srv", "head"),
            P(("dp", "head", "srv"), None),
            P(("dp", "head", "srv"), None),
        ),
        check_vma=False,
    )
```

```python
import functools

import jax
import jax.numpy as jnp
from jax import lax
from jax.experimental import pallas as pl
from jax.experimental.pallas import tpu as pltpu
from jax.sharding import PartitionSpec as P

HEAD = 128
DP = 16
QUAD = 4
BLOCKS = 3
SHARD = 640
CONTEXT = 8192
ROWS = 512
DOC_MAX = 5120
DOCS = 8
GROUPS = 8
SRVS = 4
PIECE = SHARD // GROUPS // SRVS
SCALE = HEAD**-0.5
EXP2_SCALE = SCALE * 1.4426950408889634
NEGATIVE = -1e30
NEAR = tuple(tuple(range(QUAD * q, QUAD * q + QUAD)) for q in range(DP // QUAD))
FAR = tuple(tuple(range(m, DP, QUAD)) for m in range(QUAD))

F32 = jnp.float32
BF16 = jnp.bfloat16
NT = (((1,), (1,)), ((), ()))
NN = (((1,), (0,)), ((), ()))


def dot(lhs, rhs, dims):
    return lax.dot_general(lhs, rhs, dims, preferred_element_type=F32)


def flip(block):
    size = block.shape[1]
    rows = lax.broadcasted_iota(jnp.int32, (size, size), 0)
    columns = lax.broadcasted_iota(jnp.int32, (size, size), 1)
    return dot((rows == columns).astype(BF16), block, NT)


def fold8(block, op):
    rows, cols = block.shape
    return op(block.reshape(rows // 8, 8, cols), axis=0)


def member_of(member, turn):
    return member ^ turn


def fetch(sources, targets, sems):
    copies = [
        pltpu.make_async_copy(source, target, sems.at[i])
        for i, (source, target) in enumerate(zip(sources, targets))
    ]
    for copy in copies:
        copy.start()
    return copies


def pack_kernel(
    docs_in, keys_in, values_in, out_ref, docs, keys, values, k_ref, v_ref, f_ref, sems
):
    srv = lax.axis_index("srv")
    for copy in fetch((docs_in, keys_in, values_in), (docs, keys, values), sems):
        copy.wait()
    k_ref[...] = keys[...].astype(F32)
    v_ref[...] = values[...].astype(F32)

    def mine(ref):
        piece = ref[:PIECE, :]
        for part in range(1, SRVS):
            other = ref[PIECE * part : PIECE * (part + 1), :]
            piece = jnp.where(srv == part, other, piece)
        return piece

    k, v = mine(k_ref), mine(v_ref)
    for group in range(GROUPS):
        span = slice(PIECE * group, PIECE * (group + 1))
        columns = slice(HEAD * group, HEAD * (group + 1))
        f_ref[span, :HEAD] = k[:, columns]
        f_ref[span, HEAD:] = v[:, columns]
    lanes = lax.broadcasted_iota(jnp.int32, (8, 2 * HEAD), 1)
    row = jnp.zeros((8, 2 * HEAD), F32)
    for doc in range(DOCS):
        count = jnp.sum(jnp.where(docs[...] == doc, 1.0, 0.0), axis=1, keepdims=True)
        count = jnp.sum(count, axis=0, keepdims=True).astype(jnp.int32)
        row = jnp.where(lanes == doc, (count >> 6).astype(F32), row)
        row = jnp.where(lanes == DOCS + doc, (count & 63).astype(F32), row)
    first = lax.broadcasted_iota(jnp.int32, (8, 2 * HEAD), 0) == 0
    f_ref[PIECE * GROUPS :, :] = jnp.where(first, row, 0.0)
    out_ref[...] = f_ref[...].astype(BF16)


def join_kernel(packed, queries, gradient, own_ref, qg_ref):
    own_ref[...] = packed[...].astype(F32)
    qg_ref[:, :HEAD] = queries[...]
    qg_ref[:, HEAD:] = gradient[...]


def fan_kernel(p0, p1, p2, p3, joined, out_ref, qg_ref, f_ref, slab_ref):
    rows = joined.shape[0]
    dp = lax.axis_index("dp")
    quad, member = dp // QUAD, dp % QUAD
    for turn, part in enumerate((p0, p1, p2, p3)):
        f_ref[quad ^ turn] = part[...].astype(F32)
    for group in range(GROUPS):
        for block in range(BLOCKS):
            slab_ref[group, PIECE * block : PIECE * (block + 1), :] = f_ref[
                block + 1, PIECE * group : PIECE * (group + 1), :
            ]
        slab = slab_ref[group].astype(BF16)
        for srv in range(SRVS):
            out_ref[group, srv] = slab
    count = jnp.zeros((8, 2 * HEAD), F32)
    for owner in range(1, QUAD):
        held = f_ref[owner, PIECE * GROUPS :, :]
        count += jnp.where(reached(quad, QUAD * owner + member), held, 0.0)
    qg_ref[:rows, :] = joined[...]
    qg_ref[rows:, :] = count.astype(BF16)


def fold_kernel(parts, own_ref, next_ref, far_ref, last_ref, slab_ref, f_ref):
    quad = lax.axis_index("dp") // QUAD
    for group in range(GROUPS):
        slab_ref[group] = sum(parts[group, srv].astype(F32) for srv in range(SRVS))
        for block in range(BLOCKS):
            f_ref[block, PIECE * group : PIECE * (group + 1), :] = slab_ref[
                group, PIECE * block : PIECE * (block + 1), :
            ]
    for turn, ref in enumerate((own_ref, next_ref, far_ref, last_ref)):
        owner = quad ^ turn
        ref[...] = f_ref[jnp.maximum(owner - 1, 0)].astype(BF16)

    @pl.when(quad == 0)
    def _():
        own_ref[...] = jnp.zeros(own_ref.shape, BF16)


def finish_kernel(p0, p1, p2, p3, k_ref, v_ref, f_ref):
    f_ref[...] = sum(part[...].astype(F32) for part in (p0, p1, p2, p3))
    for group in range(GROUPS):
        span = slice(PIECE * group, PIECE * (group + 1))
        columns = slice(HEAD * group, HEAD * (group + 1))
        k_ref[:, columns] = f_ref[span, :HEAD].astype(BF16)
        v_ref[:, columns] = f_ref[span, HEAD:].astype(BF16)


def forward_kernel(
    qg, slabs, e_ref, o_ref, stats_ref, active, kv, s_ref, m_ref, l_ref, slab_ref, f_ref
):
    dp = lax.axis_index("dp")
    quad, member = dp // QUAD, dp % QUAD
    qs = [qg.at[member_of(member, turn)] for turn in range(QUAD)]
    cols = o_ref.shape[2]
    keys = kv.shape[1]
    query_at = CONTEXT + 2 * cols * quad

    window_end = ((query_at + ROWS - 1) // SHARD + 1) * SHARD
    count = sum(jnp.sum(qg[who, cols:, :].astype(F32), axis=0, keepdims=True) for who in range(QUAD))
    lanes = lax.broadcasted_iota(jnp.int32, count.shape, 1)
    starts = []
    for doc in range(DOCS):
        high = jnp.sum(jnp.where((lanes >= doc) & (lanes < DOCS), count, 0.0)) * 64.0
        low = jnp.sum(
            jnp.where((lanes >= DOCS + doc) & (lanes < 2 * DOCS), count, 0.0)
        )
        starts.append(window_end - (high + low).astype(jnp.int32))
    reach = jnp.int32(0)
    for start in starts:
        reach = jnp.where(start <= query_at, jnp.maximum(reach, start), reach)
    first, last = jnp.int32(0), jnp.int32(0)
    for block in range(BLOCKS):
        shard = SHARD * (QUAD * (block + 1) + member)
        first += (shard + SHARD <= reach).astype(jnp.int32)
        last += (shard < query_at + 2 * cols).astype(jnp.int32)
    active[0] = first
    active[1] = last

    for group in range(GROUPS):
        for srv in range(SRVS):
            slab_ref[group, srv] = slabs[group, srv].astype(F32)
            at = PIECE * (SRVS * group + srv)
            for block in range(BLOCKS):
                f_ref[block, at : at + PIECE, :] = slab_ref[
                    group, srv, PIECE * block : PIECE * (block + 1), :
                ]
    for block in range(BLOCKS):
        kv[block] = f_ref[block].astype(BF16)

    pattern = lax.broadcasted_iota(jnp.int32, (keys, cols), 0) + SHARD * (QUAD + member)
    lane = lax.broadcasted_iota(jnp.int32, (1, cols), 1)
    m_ref[...] = jnp.full(m_ref.shape, NEGATIVE, F32)
    l_ref[...] = jnp.zeros(l_ref.shape, F32)
    o_ref[...] = jnp.zeros(o_ref.shape, F32)
    query_places, doc_starts = [], []
    for turn in range(QUAD):
        query_place = query_at + (cols // 2) * member_of(member, turn) + lane // 2
        doc_start = jnp.zeros_like(query_place)
        for start in starts:
            doc_start = jnp.where(start <= query_place, jnp.maximum(doc_start, start), doc_start)
        query_places.append(query_place)
        doc_starts.append(doc_start)

    def scores(t, carry):
        k = kv[t, :, :HEAD]
        key_place = pattern + QUAD * SHARD * t
        for turn in range(QUAD):
            span = pl.ds(turn * cols, cols)
            s = dot(k, qs[turn][:cols, :HEAD], NT)
            since = (key_place - doc_starts[turn]).astype(jnp.uint32)
            allowed = since <= (query_places[turn] - doc_starts[turn]).astype(jnp.uint32)
            s = jnp.where(allowed, s, NEGATIVE)
            s_ref[t, :, span] = s
            m_ref[turn] = jnp.maximum(m_ref[turn], fold8(s, jnp.max))
        return carry

    lax.fori_loop(first, last, scores, 0)
    tops = [jnp.max(m_ref[turn], axis=0, keepdims=True) for turn in range(QUAD)]

    def weigh(t, carry):
        v = flip(kv[t, :, HEAD:]).astype(BF16)
        for turn in range(QUAD):
            span = pl.ds(turn * cols, cols)
            e = jnp.exp2((s_ref[t, :, span] - tops[turn]) * EXP2_SCALE)
            l_ref[turn] += fold8(e, jnp.sum)
            e = e.astype(BF16)
            e_ref[t, :, span] = e
            o_ref[turn] += dot(v, e, NN)
        return carry

    lax.fori_loop(first, last, weigh, 0)
    for turn in range(QUAD):
        tile = member_of(member, turn)
        gradient = flip(qs[turn][:cols, HEAD:])
        norm = jnp.sum(l_ref[turn], axis=0, keepdims=True)
        delta = jnp.sum(gradient * o_ref[turn], axis=0, keepdims=True)
        for copy in range(QUAD):
            stats_ref[copy, pl.ds(tile, 1), :] = tops[turn]
            stats_ref[copy, pl.ds(QUAD + tile, 1), :] = norm
            stats_ref[copy, pl.ds(2 * QUAD + tile, 1), :] = delta
            stats_ref[copy, pl.ds(3 * QUAD + tile, 1), :] = jnp.zeros_like(norm)


def backward_kernel(
    active, qg, kv, e_ref, o_ref, stats, oq0, oq1, oq2, oq3, dkv_ref, dq_ref, f_ref, slab_ref
):
    member = lax.axis_index("dp") % QUAD
    first, last = active[0], active[1]
    qs = [qg.at[member_of(member, turn)] for turn in range(QUAD)]
    oqs = (oq0, oq1, oq2, oq3)
    cols = o_ref.shape[2]
    keys = kv.shape[1]
    dq_ref[...] = jnp.zeros(dq_ref.shape, F32)
    shares, deltas = [], []
    for turn in range(QUAD):
        tile = member_of(member, turn)
        row = lambda who, kind: stats[who, pl.ds(kind * QUAD + tile, 1), :]
        top = functools.reduce(jnp.maximum, [row(who, 0) for who in range(QUAD)])
        weights = [jnp.exp2((row(who, 0) - top) * EXP2_SCALE) for who in range(QUAD)]
        norm = sum(weights[who] * row(who, 1) for who in range(QUAD))
        deltas.append(sum(weights[who] * row(who, 2) for who in range(QUAD)) / norm)
        shares.append(jnp.exp2((row(member, 0) - top) * EXP2_SCALE) / norm)

    def clear(t, carry):
        f_ref[t] = jnp.zeros((keys, 2 * HEAD), F32)
        return carry

    lax.fori_loop(0, first, clear, 0)
    lax.fori_loop(last, BLOCKS, clear, 0)

    def grads(t, carry):
        k = kv[t, :, :HEAD]
        v = kv[t, :, HEAD:]
        kt = flip(k).astype(BF16)
        dk = jnp.zeros((keys, HEAD), F32)
        dv = jnp.zeros((keys, HEAD), F32)
        for turn in range(QUAD):
            q, gradient = qs[turn][:cols, :HEAD], qs[turn][:cols, HEAD:]
            p = e_ref[t, :, pl.ds(turn * cols, cols)].astype(F32) * shares[turn]
            ds = (p * (dot(v, gradient, NT) - deltas[turn])).astype(BF16)
            dv += dot(p.astype(BF16), gradient, NN)
            dk += dot(ds, q, NN)
            dq_ref[turn] += dot(kt, ds, NN)
        f_ref[t, :, :HEAD] = dk * SCALE
        f_ref[t, :, HEAD:] = dv
        return carry

    lax.fori_loop(first, last, grads, 0)
    for turn in range(QUAD):
        oqs[turn][:, :HEAD] = flip((o_ref[turn] * shares[turn]).astype(BF16)).astype(BF16)
        oqs[turn][:, HEAD:] = flip((dq_ref[turn] * SCALE).astype(BF16)).astype(BF16)
    for group in range(GROUPS):
        for srv in range(SRVS):
            at = PIECE * (SRVS * group + srv)
            for block in range(BLOCKS):
                slab_ref[group, srv, PIECE * block : PIECE * (block + 1), :] = f_ref[
                    block, at : at + PIECE, :
                ]
            dkv_ref[group, srv] = slab_ref[group, srv].astype(BF16)


def exchange(block, axis, groups=None):
    return lax.all_to_all(block, axis, 0, 0, tiled=True, axis_index_groups=groups)


def swap(block, turn):
    return lax.ppermute(block, "dp", [(place, place ^ turn) for place in range(DP)])


def reached(quad, shard):
    first = CONTEXT + ROWS * quad
    return (first - (DOC_MAX - 1) < SHARD * (shard + 1)) & (SHARD * shard < first + ROWS)


def hand_out(block, turn):
    pairs = []
    for owner in range(1, QUAD):
        quad = owner ^ turn
        for m in range(QUAD):
            if reached(quad, QUAD * owner + m):
                pairs.append((QUAD * owner + m, QUAD * quad + m))
    return lax.ppermute(block, "dp", pairs)


def carry_on(block, turn):
    pairs = []
    for quad in range(QUAD):
        owner = quad ^ turn
        for m in range(QUAD) if owner else ():
            if reached(quad, QUAD * owner + m):
                pairs.append((QUAD * quad + m, QUAD * owner + m))
    return lax.ppermute(block, "dp", pairs)


def local(queries, keys, values, output_gradient, doc_ids):
    rows = queries.shape[0] * queries.shape[1]
    part = GROUPS * PIECE
    wide = 2 * HEAD
    vmem = pl.BlockSpec(memory_space=pltpu.VMEM)
    smem = pl.BlockSpec(memory_space=pltpu.SMEM)
    params = pltpu.CompilerParams(vmem_limit_bytes=30 * 1024 * 1024)
    roomy = pltpu.CompilerParams(vmem_limit_bytes=60 * 1024 * 1024)
    call = functools.partial(pl.pallas_call, compiler_params=params)
    slabs_shape = (GROUPS, SRVS, BLOCKS * PIECE, wide)

    hbm = pl.BlockSpec(memory_space=pltpu.HBM)
    sources = (doc_ids.reshape(-1, 128), keys, values)
    packed = pl.pallas_call(
        pack_kernel,
        out_shape=jax.ShapeDtypeStruct((part + 8, wide), BF16),
        in_specs=[hbm] * 3,
        out_specs=vmem,
        scratch_shapes=[pltpu.VMEM(x.shape, x.dtype) for x in sources]
        + [
            pltpu.VMEM(keys.shape, F32),
            pltpu.VMEM(values.shape, F32),
            pltpu.VMEM((part + 8, wide), F32),
            pltpu.SemaphoreType.DMA((3,)),
        ],
        compiler_params=roomy,
        name="pack",
    )(*sources)
    parts = [hand_out(packed, turn) for turn in (2, 3, 1)]
    own, joined = call(
        join_kernel,
        out_shape=(
            jax.ShapeDtypeStruct((part + 8, wide), F32),
            jax.ShapeDtypeStruct((rows, wide), BF16),
        ),
        in_specs=[vmem] * 3,
        out_specs=(vmem, vmem),
        name="join",
    )(packed, queries.reshape(rows, HEAD), output_gradient.reshape(rows, HEAD))
    slabs, qg = pl.pallas_call(
        fan_kernel,
        out_shape=(
            jax.ShapeDtypeStruct(slabs_shape, BF16),
            jax.ShapeDtypeStruct((rows + 8, wide), BF16),
        ),
        in_specs=[vmem] * (QUAD + 1),
        out_specs=(vmem, vmem),
        scratch_shapes=[
            pltpu.VMEM((QUAD, part + 8, wide), F32),
            pltpu.VMEM((GROUPS, BLOCKS * PIECE, wide), F32),
        ],
        compiler_params=params,
        name="fan",
    )(own, parts[2], parts[0], parts[1], joined)
    flat = (GROUPS * SRVS, BLOCKS * PIECE, wide)
    slabs = exchange(slabs.reshape(flat), ("head", "srv")).reshape(slabs_shape)
    qg = lax.all_gather(qg, "dp", axis=0, axis_index_groups=NEAR)

    e, o, stats, active, kv = call(
        forward_kernel,
        out_shape=(
            jax.ShapeDtypeStruct((BLOCKS, SHARD, QUAD * rows), BF16),
            jax.ShapeDtypeStruct((QUAD, HEAD, rows), F32),
            jax.ShapeDtypeStruct((QUAD, 4 * QUAD, rows), F32),
            jax.ShapeDtypeStruct((2,), jnp.int32),
            jax.ShapeDtypeStruct((BLOCKS, SHARD, wide), BF16),
        ),
        in_specs=[vmem] * 2,
        out_specs=(vmem, vmem, vmem, smem, vmem),
        scratch_shapes=[
            pltpu.VMEM((BLOCKS, SHARD, QUAD * rows), F32),
            pltpu.VMEM((QUAD, 8, rows), F32),
            pltpu.VMEM((QUAD, 8, rows), F32),
            pltpu.VMEM(slabs_shape, F32),
            pltpu.VMEM((BLOCKS, SHARD, wide), F32),
        ],
        name="forward",
    )(qg, slabs)
    stats = exchange(stats.reshape(QUAD * 4 * QUAD, rows), "dp", NEAR)
    stats = stats.reshape(QUAD, 4 * QUAD, rows)
    *oqs, dkv = call(
        backward_kernel,
        out_shape=(
            *[jax.ShapeDtypeStruct((rows, wide), BF16)] * QUAD,
            jax.ShapeDtypeStruct(slabs_shape, BF16),
        ),
        in_specs=[smem] + [vmem] * 5,
        out_specs=(vmem,) * 5,
        scratch_shapes=[
            pltpu.VMEM((QUAD, HEAD, rows), F32),
            pltpu.VMEM((BLOCKS, SHARD, wide), F32),
            pltpu.VMEM(slabs_shape, F32),
        ],
        name="backward",
    )(active, qg, kv, e, o, stats)

    oqs = [swap(oqs[turn], turn) for turn in (3, 2, 1)] + [oqs[0]]
    dkv = exchange(dkv.reshape(flat), ("head", "srv"))
    dkv, oqs = lax.optimization_barrier((dkv, oqs))
    dkv = call(
        fold_kernel,
        out_shape=(jax.ShapeDtypeStruct((part, wide), BF16),) * QUAD,
        in_specs=[vmem],
        out_specs=(vmem,) * QUAD,
        scratch_shapes=[
            pltpu.VMEM((GROUPS, BLOCKS * PIECE, wide), F32),
            pltpu.VMEM((BLOCKS, part, wide), F32),
        ],
        name="fold",
    )(dkv.reshape(slabs_shape))
    dkv = [carry_on(dkv[turn], turn) for turn in (2, 3, 1)] + [dkv[0]]
    k_grad, v_grad = call(
        finish_kernel,
        out_shape=(jax.ShapeDtypeStruct((PIECE, GROUPS * HEAD), BF16),) * 2,
        in_specs=[vmem] * QUAD,
        out_specs=(vmem, vmem),
        scratch_shapes=[pltpu.VMEM((part, wide), F32)],
        name="finish",
    )(*dkv)

    oq = sum(x.astype(F32) for x in oqs).astype(BF16)
    attention = oq[:, :HEAD].reshape(queries.shape)
    q_grad = oq[:, HEAD:].reshape(queries.shape)
    return attention, q_grad, k_grad, v_grad


def solution(mesh):
    placed = (
        P("dp", "srv", "head"),
        P(("dp", "head"), None),
        P(("dp", "head"), None),
        P("dp", "srv", "head"),
        P("dp"),
    )
    return jax.shard_map(
        local,
        mesh=mesh,
        in_specs=placed,
        out_specs=(
            P("dp", "srv", "head"),
            P("dp", "srv", "head"),
            P(("dp", "head", "srv"), None),
            P(("dp", "head", "srv"), None),
        ),
        check_vma=False,
    )
```
